256 devices in a mesh: grp: 4 (over y), lst: 64 (over x, z, core).
Axes of the slice: x: 4, y: 4, z: 8, core: 2. Of those that a mesh axis runs over, the one named last changes fastest.
Arguments:
- new_rows: bfloat16 [131072, 1024], P(('grp', 'lst')), may hold values from -6 to 6
- list_ids: int32 [131072], P(('grp', 'lst')), may hold values from 0 to 65535, as said below
- rotation: bfloat16 [1024, 1024], replicated, may hold values from -0.1875 to 0.1875
- centroids: float32 [65536, 1024], P('lst'), may hold values from -6 to 6
- prior_counts: float32 [65536], P('lst'), may hold values from 1 to 10
Outputs:
- new_centroids: float32 [65536, 1024], P('lst')
- residuals: bfloat16 [131072, 1024], P(('grp', 'lst'))
The draws below stay inside these ranges and needn't reach their ends.
Inputs may be any that keep to these rules, and one draw needn't show every extreme that they name: `list_ids`: on one device, at most 32 rows name lists of one owner (lists o * 1024 to (o + 1) * 1024 - 1); in every draw each group has an owner that gets exactly 32 rows from every device of the group.
All inputs are finite; a program needn't handle non-finite values.
Results may differ from the reference program's by a relative error of at most 0.009.
Values may be sent and summed in bfloat16 or wider, within the bound.
No kernel may reach another device: no remote copies, remote signals or barrier semaphores. Data moves between devices by JAX's collectives and lax.ppermute only.
A program may use at most 128 MiB of HBM per device.

```python
import math
import jax
import jax.numpy as jnp

D = 1024
LISTS_DEV = 1024
ROWS_DEV = 512
CAP = 32
LISTS = 65536
TOKENS = 131072
N_GRP = 4
N_LST = 64


def draw_list_ids(key, part):
    key = jax.random.fold_in(key, 11)
    keys = jax.random.split(key, 5)
    block_count = N_GRP * N_LST
    hot_owner = jax.random.randint(keys[0], (N_GRP,), 0, N_LST)
    hot_block = jnp.repeat(hot_owner, N_LST)
    offset_pool = jnp.repeat(jnp.arange(1, N_LST, dtype=jnp.int32), CAP)

    def pick_rest(subkey):
        return jax.random.permutation(subkey, offset_pool)[:ROWS_DEV - CAP]
    rest_offsets = jax.vmap(pick_rest)(jax.random.split(keys[1], block_count))
    offsets = jnp.concatenate([jnp.zeros((block_count, CAP), jnp.int32), rest_offsets], axis=1)
    owners = (hot_block[:, None] + offsets) % N_LST

    def shuffle_row(subkey, values):
        return values[jax.random.permutation(subkey, ROWS_DEV)]
    owners = jax.vmap(shuffle_row)(jax.random.split(keys[2], block_count), owners)
    first_pick = jax.random.randint(keys[3], (block_count, ROWS_DEV), 0, LISTS_DEV)
    second_pick = jax.random.randint(keys[4], (block_count, ROWS_DEV), 0, LISTS_DEV)
    local_list = jnp.minimum(first_pick, second_pick)
    return (owners * LISTS_DEV + local_list).reshape(-1).astype(jnp.int32)


def block_levels(stream_key, extent, cuts, least, largest):
    def one(position, blocks):
        steps = jax.random.uniform(jax.random.fold_in(jax.random.fold_in(stream_key, 6), position), (blocks,), jnp.float32, least / len(cuts), largest / len(cuts))
        return jnp.repeat(jnp.exp(steps), extent[position] // blocks).reshape((-1,) + (1,) * (len(extent) - position - 1))

    gain = one(*cuts[0])
    for cut in cuts[1:]:
        gain = gain * one(*cut)
    return gain


def gaussian(stream_key, extent, deviation, limit, shards=(), kind=jnp.bfloat16):
    values = jax.random.normal(stream_key, extent, jnp.float32) * deviation
    if len(shards) > 0:
        values = block_levels(stream_key, extent, shards, -0.22, 0.18) * values
    return jnp.clip(values, min=-limit, max=limit).astype(kind)


def setup_inputs(seed: int = 0) -> dict:
    seeds = jax.random.split(jax.random.key(seed), 6)
    new_rows = gaussian(seeds[0], (TOKENS, D), 1.0, 6.0, ((0, 256),))
    list_ids = draw_list_ids(jax.random.fold_in(seeds[5], 71), 0)
    rotation = gaussian(seeds[2], (D, D), D ** -0.5, 0.1875)
    centroids = gaussian(seeds[3], (LISTS, D), 1.0, 6.0, ((0, 64),), jnp.float32)
    prior_counts = jnp.clip(jnp.exp(math.log(10.0) - 2.3025851 * jax.random.uniform(seeds[4], (LISTS,), jnp.float32) ** block_levels(seeds[4], (LISTS,), ((0, 64),), -0.2, 0.2)), 1.0, 10.0)
    return dict(new_rows=new_rows, list_ids=list_ids, rotation=rotation, centroids=centroids, prior_counts=prior_counts)


def reference(new_rows, list_ids, rotation, centroids, prior_counts):
    rotated = jnp.dot(new_rows, rotation, preferred_element_type=jnp.float32).astype(jnp.bfloat16)
    lookup = jnp.take(centroids, list_ids, axis=0)
    residuals = (rotated.astype(jnp.float32) - lookup).astype(jnp.bfloat16)
    list_sums = jax.ops.segment_sum(residuals.astype(jnp.float32), list_ids, num_segments=LISTS)
    list_counts = jax.ops.segment_sum(jnp.ones(list_ids.shape, jnp.float32), list_ids, num_segments=LISTS)
    new_centroids = centroids + list_sums / (prior_counts + list_counts)[:, None]
    return new_centroids, residuals
```

```python
import functools

import jax
import jax.numpy as jnp
from jax import lax
from jax.experimental import pallas as pl
from jax.experimental.pallas import tpu as pltpu
from jax.sharding import PartitionSpec as P

CONTRACT_LAST = (((1,), (1,)), ((), ()))
CONTRACT_FIRST = (((0,), (0,)), ((), ()))
BF16 = jnp.bfloat16
F32 = jnp.float32


def slots_kernel(peers, capacity, per_owner, ids_ref, slot_ref, codes_ref):
    ids = ids_ref[...]
    rows = ids.shape[1]
    owner = ids // per_owner
    local = ids - owner * per_owner + 1
    member = lax.broadcasted_iota(jnp.int32, (peers, rows), 0) == owner
    member_f = jnp.where(member, 1.0, 0.0).astype(F32)
    earlier = lax.broadcasted_iota(jnp.int32, (rows, rows), 0) < lax.broadcasted_iota(
        jnp.int32, (rows, rows), 1
    )
    before = jnp.dot(
        member_f.astype(BF16),
        jnp.where(earlier, 1.0, 0.0).astype(BF16),
        preferred_element_type=F32,
    )
    rank = jnp.sum(jnp.where(member, before, 0.0), axis=0, keepdims=True).astype(jnp.int32)
    slot_ref[...] = owner * capacity + rank
    at_rank = lax.broadcasted_iota(jnp.int32, (capacity, rows), 0) == rank
    at_rank = jnp.where(at_rank, 1.0, 0.0).astype(BF16)
    high = local // 32
    low = local - high * 32

    def place(value):
        spread = jnp.where(member, value.astype(F32), 0.0).astype(BF16)
        return lax.dot_general(spread, at_rank, CONTRACT_LAST, preferred_element_type=F32)

    codes_ref[...] = (place(high) * 32.0 + place(low)).astype(jnp.int32)


def pack_kernel(block, slot_ref, rows_ref, rotation_ref, send_ref, rotated_ref):
    step = pl.program_id(0)

    @pl.when(step == 0)
    def _():
        rotated_ref[...] = jnp.dot(
            rows_ref[...], rotation_ref[...], preferred_element_type=F32
        ).astype(BF16)

    rows = rows_ref.shape[0]
    chosen = lax.broadcasted_iota(jnp.int32, (block, rows), 0) + step * block == slot_ref[...]
    send_ref[...] = jnp.dot(
        jnp.where(chosen, 1.0, 0.0).astype(BF16), rotated_ref[...], preferred_element_type=F32
    ).astype(BF16)


def unpack_kernel(slot_ref, returned_ref, out_ref, chosen_ref):
    slots, rows = chosen_ref.shape

    @pl.when(pl.program_id(0) == 0)
    def _():
        chosen = lax.broadcasted_iota(jnp.int32, (slots, rows), 0) == slot_ref[...]
        chosen_ref[...] = jnp.where(chosen, 1.0, 0.0).astype(BF16)

    out_ref[...] = lax.dot_general(
        chosen_ref[...], returned_ref[...], CONTRACT_FIRST, preferred_element_type=F32
    ).astype(BF16)


def whole(shape):
    return pl.BlockSpec(shape, lambda i: (0,) * len(shape))


def make_slots(list_ids, peers, capacity, per_owner):
    rows = list_ids.shape[0]
    return pl.pallas_call(
        functools.partial(slots_kernel, peers, capacity, per_owner),
        out_shape=(
            jax.ShapeDtypeStruct((1, rows), jnp.int32),
            jax.ShapeDtypeStruct((peers, capacity), jnp.int32),
        ),
        name="slots",
    )(list_ids.reshape(1, rows))


def pack(slot, new_rows, rotation, slots):
    rows, width = new_rows.shape
    block = 256
    return pl.pallas_call(
        functools.partial(pack_kernel, block),
        grid=(slots // block,),
        in_specs=[whole(slot.shape), whole(new_rows.shape), whole(rotation.shape)],
        out_specs=pl.BlockSpec((block, width), lambda i: (i, 0)),
        out_shape=jax.ShapeDtypeStruct((slots, width), BF16),
        scratch_shapes=[pltpu.VMEM((rows, width), BF16)],
        compiler_params=pltpu.CompilerParams(vmem_limit_bytes=40 * 2**20),
        name="pack",
    )(slot, new_rows, rotation)


def unpack(slot, returned):
    rows = slot.shape[1]
    slots, width = returned.shape
    block = 256
    return pl.pallas_call(
        unpack_kernel,
        grid=(width // block,),
        in_specs=[whole(slot.shape), pl.BlockSpec((slots, block), lambda i: (0, i))],
        out_specs=pl.BlockSpec((rows, block), lambda i: (0, i)),
        out_shape=jax.ShapeDtypeStruct((rows, width), BF16),
        scratch_shapes=[pltpu.VMEM((slots, rows), BF16)],
        compiler_params=pltpu.CompilerParams(vmem_limit_bytes=40 * 2**20),
        name="unpack",
    )(slot, returned)


def shards(new_rows, list_ids, rotation, centroids, prior_counts):
    peers = lax.axis_size("lst")
    row_count, width = new_rows.shape
    per_owner = centroids.shape[0]
    capacity = max(2, 4 * row_count // peers)
    slots = peers * capacity
    slot, codes = make_slots(list_ids, peers, capacity, per_owner)
    arrived_codes = lax.all_to_all(codes, "lst", split_axis=0, concat_axis=0, tiled=True)
    send_rows = pack(slot, new_rows, rotation, slots).reshape(peers, capacity, width)
    arrived = lax.all_to_all(send_rows, "lst", split_axis=0, concat_axis=0, tiled=True)
    local = arrived_codes.reshape(slots) - 1
    lookup = jnp.take(centroids, jnp.maximum(local, 0), axis=0)
    residual = jnp.where(
        (local >= 0)[:, None], arrived.reshape(slots, width).astype(F32) - lookup, 0.0
    ).astype(BF16)
    returned = lax.all_to_all(
        residual.reshape(peers, capacity, width), "lst", split_axis=0, concat_axis=0, tiled=True
    )
    member = (jnp.arange(per_owner, dtype=jnp.int32)[:, None] == local[None, :]).astype(BF16)
    list_sums = jnp.dot(member, residual, preferred_element_type=F32)
    list_counts = jnp.sum(member, axis=1, dtype=F32)
    total_sums = lax.psum(list_sums.astype(BF16), "grp").astype(F32)
    total_counts = lax.psum(list_counts, "grp")
    new_centroids = centroids + total_sums / (prior_counts + total_counts)[:, None]
    residuals = unpack(slot, returned.reshape(slots, width))
    return (new_centroids, residuals)


def solution(mesh):
    return jax.shard_map(
        shards,
        mesh=mesh,
        in_specs=(P(("grp", "lst"), None), P(("grp", "lst")), P(), P("lst", None), P("lst")),
        out_specs=(P("lst", None), P(("grp", "lst"), None)),
        check_vma=False,
    )
```

```python
import functools

import jax
import jax.numpy as jnp
from jax import lax
from jax.experimental import pallas as pl
from jax.experimental.pallas import tpu as pltpu
from jax.sharding import Mesh, PartitionSpec as P

CONTRACT_LAST = (((1,), (1,)), ((), ()))
CONTRACT_FIRST = (((0,), (0,)), ((), ()))
BF16 = jnp.bfloat16
F32 = jnp.float32
I32 = jnp.int32
CORES = 2
SPARE = 32
EXTRA = 128
FULL = 4096


def hot(mask):
    return jnp.where(mask, 1.0, 0.0).astype(BF16)


def iota(shape, dim):
    return lax.broadcasted_iota(I32, shape, dim)


def whole(shape):
    return pl.BlockSpec(shape, lambda *i: (0,) * len(shape))


def params():
    return pltpu.CompilerParams(vmem_limit_bytes=48 * 2**20)


def assign_kernel(groups, chips, capacity, per_chip, me_ref, ids_ref, place_ref, spare_ref, codes_ref):
    me = me_ref[0]
    rows = ids_ref.shape[1]
    earlier = hot(iota((rows, rows), 0) < iota((rows, rows), 1))
    cap = float(capacity)
    ids = [ids_ref[pl.ds(lax.rem(me - j + groups, groups), 1), :] for j in range(groups)]
    chip = [v // per_chip for v in ids]
    local = [v - c * per_chip + 1 for v, c in zip(ids, chip)]
    member = [iota((chips, rows), 0) == c for c in chip]
    member_f = [jnp.where(m, 1.0, 0.0) for m in member]
    before = jnp.dot(
        jnp.concatenate(member_f, axis=0).astype(BF16), earlier, preferred_element_type=F32
    )
    count = [jnp.sum(m, axis=1, keepdims=True) for m in member_f]
    free = [jnp.maximum(cap - n, 0.0) for n in count]
    over = [jnp.maximum(n - cap, 0.0) for n in count]
    free_at, over_at = [jnp.zeros_like(count[0])], [jnp.zeros_like(count[0])]
    for j in range(groups):
        free_at.append(free_at[-1] + free[j])
        over_at.append(over_at[-1] + over[j])
    lost = jnp.sum(jnp.maximum(over_at[-1] - free_at[-1], 0.0), axis=0, keepdims=True)
    target, slot = [], []
    for j in range(groups):
        rank = before[j * chips : (j + 1) * chips]
        stays = rank < cap
        entry = rank - cap + over_at[j]
        goes_to = jnp.full_like(rank, -1.0)
        lands = jnp.zeros_like(rank)
        for i in range(groups):
            inside = (entry >= free_at[i]) & (entry < free_at[i + 1])
            goes_to = jnp.where(inside, float(i), goes_to)
            lands = jnp.where(inside, count[i] + entry - free_at[i], lands)
        goes_to = jnp.where(stays, float(j), goes_to)
        lands = jnp.where(stays, rank, lands)
        target.append(jnp.sum(jnp.where(member[j], goes_to, 0.0), axis=0, keepdims=True).astype(I32))
        slot.append(jnp.sum(jnp.where(member[j], lands, 0.0), axis=0, keepdims=True).astype(I32))
    moves = [
        jnp.where(target[j] == i, 1.0, 0.0) if i != j else jnp.zeros((1, rows), F32)
        for j in range(groups)
        for i in range(groups)
    ]
    moves = jnp.concatenate(moves, axis=0)
    queue = jnp.dot(moves.astype(BF16), earlier, preferred_element_type=F32)
    totals = jnp.sum(moves, axis=1, keepdims=True)
    lost = lost + jnp.sum(jnp.maximum(totals - float(SPARE), 0.0), axis=0, keepdims=True)

    place = jnp.full((1, rows), -1, I32)
    spare = jnp.full((1, rows), -1, I32)
    arriving = jnp.zeros((8, EXTRA), F32)
    codes = jnp.zeros(codes_ref.shape, F32)
    peers = codes_ref.shape[0]
    for j in range(groups):
        mine = me == j
        flat = chip[j] * capacity + slot[j]
        place = jnp.where(mine & (target[j] == j), flat, place)
        for i in range(groups):
            if i == j:
                continue
            shift = (i - j) % groups - 1
            at = queue[j * groups + i : j * groups + i + 1].astype(I32) + shift * SPARE
            leaves = target[j] == i
            spare = jnp.where(mine & leaves, at, spare)
            to_me = hot((iota((EXTRA, rows), 0) == at) & leaves & (me == i))
            value = flat + 1
            high = value // 32
            low = value - high * 32
            pair = jnp.where(iota((8, rows), 0) == 0, high, low).astype(F32).astype(BF16)
            arriving = arriving + lax.dot_general(
                pair, to_me, CONTRACT_LAST, preferred_element_type=F32
            )
        at_slot = hot(iota((capacity, rows), 0) == slot[j])
        served = (iota((peers, rows), 0) // CORES == chip[j]) & (target[j] == me)
        high = local[j] // 32
        low = local[j] - high * 32
        for value, factor in ((high, 32.0), (low, 1.0)):
            spread = jnp.where(served, value.astype(F32), 0.0).astype(BF16)
            codes = codes + factor * lax.dot_general(
                spread, at_slot, CONTRACT_LAST, preferred_element_type=F32
            )
    place_ref[:, :rows] = place
    place_ref[:, rows:] = (arriving[0:1] * 32.0 + arriving[1:2]).astype(I32) - 1
    spare_ref[...] = spare
    codes_ref[...] = (codes + jnp.where(lost > 0.0, float(FULL), 0.0)).astype(I32)


def rotate_kernel(spare_ref, rows_ref, rotation_ref, rotated_ref, leaving_ref):
    rotated = jnp.dot(rows_ref[...], rotation_ref[...], preferred_element_type=F32).astype(BF16)
    rotated_ref[...] = rotated
    chosen = hot(iota((leaving_ref.shape[0], rotated.shape[0]), 0) == spare_ref[...])
    leaving_ref[...] = jnp.dot(chosen, rotated, preferred_element_type=F32).astype(BF16)


def pack_kernel(block, place_ref, rotated_ref, a_ref, b_ref, c_ref, send_ref, all_ref):
    step = pl.program_id(0)
    rows = rotated_ref.shape[0]

    @pl.when(step == 0)
    def _():
        all_ref[:rows] = rotated_ref[...]
        for k, ref in enumerate((a_ref, b_ref, c_ref)):
            all_ref[rows + k * SPARE : rows + (k + 1) * SPARE] = ref[...]
        all_ref[rows + 3 * SPARE :] = jnp.zeros((EXTRA - 3 * SPARE, all_ref.shape[1]), BF16)

    chosen = hot(iota((block, all_ref.shape[0]), 0) + step * block == place_ref[...])
    send_ref[...] = jnp.dot(chosen, all_ref[...], preferred_element_type=F32).astype(BF16)


def pick_kernel(place_ref, returned_ref, out_ref):
    chosen = hot(iota((returned_ref.shape[0], place_ref.shape[1]), 0) == place_ref[...])
    out_ref[...] = lax.dot_general(
        chosen, returned_ref[...], CONTRACT_FIRST, preferred_element_type=F32
    ).astype(BF16)


def join_kernel(spare_ref, own_ref, a_ref, b_ref, c_ref, out_ref):
    total = own_ref[...].astype(F32)
    spare = spare_ref[...]
    back = jnp.concatenate([a_ref[...], b_ref[...], c_ref[...]], axis=0)
    chosen = hot(iota((3 * SPARE, spare.shape[1]), 0) == spare)
    total = total + lax.dot_general(chosen, back, CONTRACT_FIRST, preferred_element_type=F32)
    out_ref[...] = total.astype(BF16)


def shape(dims, dtype):
    return jax.ShapeDtypeStruct(dims, dtype)


def assign(me, ids, chips, capacity, per_chip):
    groups, rows = ids.shape
    return pl.pallas_call(
        functools.partial(assign_kernel, groups, chips, capacity, per_chip),
        in_specs=[pl.BlockSpec(memory_space=pltpu.SMEM), pl.BlockSpec(memory_space=pltpu.VMEM)],
        out_shape=(
            shape((1, rows + EXTRA), I32),
            shape((1, rows), I32),
            shape((chips * CORES, capacity), I32),
        ),
        compiler_params=params(),
        name="assign",
    )(me, ids)


def rotate(spare, new_rows, rotation):
    rows, width = new_rows.shape
    return pl.pallas_call(
        rotate_kernel,
        out_shape=(shape((rows, width), BF16), shape((EXTRA, width), BF16)),
        compiler_params=params(),
        name="rotate",
    )(spare, new_rows, rotation)


def pack(place, rotated, guests, slots):
    rows, width = rotated.shape
    block = 256
    return pl.pallas_call(
        functools.partial(pack_kernel, block),
        grid=(slots // block,),
        in_specs=[whole(place.shape), whole(rotated.shape)] + [whole(g.shape) for g in guests],
        out_specs=pl.BlockSpec((block, width), lambda i: (i, 0)),
        out_shape=shape((slots, width), BF16),
        scratch_shapes=[pltpu.VMEM((rows + EXTRA, width), BF16)],
        compiler_params=params(),
        name="pack",
    )(place, rotated, *guests)


def pick(place, returned):
    slots, width = returned.shape
    count = place.shape[1]
    block = 256
    return pl.pallas_call(
        pick_kernel,
        grid=(width // block,),
        in_specs=[whole(place.shape), pl.BlockSpec((slots, block), lambda i: (0, i))],
        out_specs=pl.BlockSpec((count, block), lambda i: (0, i)),
        out_shape=shape((count, width), BF16),
        compiler_params=params(),
        name="pick",
    )(place, returned)


def join(spare, own, guests):
    return pl.pallas_call(
        join_kernel,
        out_shape=shape(own.shape, BF16),
        compiler_params=params(),
        name="join",
    )(spare, own, *guests)


def around(value, axis, shift):
    count = lax.axis_size(axis)
    return lax.ppermute(value, axis, [(i, (i + shift) % count) for i in range(count)])


def exchange(value, axes):
    return lax.all_to_all(value, axes, split_axis=0, concat_axis=0, tiled=True)


def by_chip(place, spare, codes, rotated, guests, list_ids, centroids, prior_counts):
    groups, chips = lax.axis_size("grp"), lax.axis_size("chip")
    core = lax.axis_index("core")
    per_owner, width = centroids.shape
    rows = list_ids.shape[0]
    capacity = codes.shape[2]
    slots = chips * capacity
    send = pack(place, rotated, guests, slots).reshape(chips, capacity, width)
    arrived = exchange(send, "chip").reshape(slots, width)
    table = jnp.concatenate([centroids, around(centroids, "core", 1)], axis=0)
    local = codes - 1
    filled = local >= 0
    near = jnp.where(local // per_owner == core, local % per_owner, per_owner + local % per_owner)
    near = jnp.where(filled, near, -1)
    lists = jnp.arange(per_owner, dtype=I32)[:, None]
    list_counts = jnp.sum(lists == near.reshape(1, -1), axis=1, dtype=F32)
    total_counts = prior_counts + lax.psum(list_counts, "grp")
    here = lax.dynamic_index_in_dim(near, core, axis=1, keepdims=False).reshape(slots)
    lookup = jnp.take(table, jnp.maximum(here, 0), axis=0)
    residual = jnp.where((here >= 0)[:, None], arrived.astype(F32) - lookup, 0.0).astype(BF16)
    residual = lax.optimization_barrier(residual)
    returned = exchange(residual.reshape(chips, capacity, width), "chip").reshape(slots, width)
    far_sums = jnp.dot(
        (lists + per_owner == here[None, :]).astype(BF16), residual, preferred_element_type=F32
    ).astype(BF16)
    far_sums = around(far_sums, "core", 1)
    sums = jnp.dot((lists == here[None, :]).astype(BF16), residual, preferred_element_type=F32)
    sums = (sums + far_sums.astype(F32)).astype(BF16)
    total_sums = lax.psum(sums, "grp").astype(F32)
    new_centroids = centroids + total_sums / total_counts[:, None]
    back = pick(place[:, rows:], returned)
    back = [around(back[k * SPARE : (k + 1) * SPARE], "grp", groups - k - 1) for k in range(3)]
    own = pick(place[:, :rows], returned)
    return new_centroids, join(spare, own, back)


def by_owner(place, spare, codes, rotated, guests, list_ids, centroids, prior_counts):
    lst = ("chip", "core")
    peers = lax.axis_size("chip") * CORES
    rows, width = rotated.shape
    per_owner = centroids.shape[0]
    capacity = max(2, 4 * rows // peers)
    slots = peers * capacity
    owner = list_ids // per_owner
    table = (owner[:, None] == jnp.arange(peers, dtype=I32)[None, :]).astype(I32)
    rank = jnp.sum(table * (jnp.cumsum(table, axis=0) - 1), axis=1)
    where_to = owner * capacity + rank
    source = jnp.full((slots,), rows, I32).at[where_to].set(jnp.arange(rows, dtype=I32))
    filled = source < rows
    safe = jnp.minimum(source, rows - 1)
    send = jnp.where(filled[:, None], jnp.take(rotated, safe, axis=0), jnp.zeros((), BF16))
    send_ids = jnp.where(filled, jnp.take(list_ids, safe, axis=0), -1)
    arrived = exchange(send.reshape(peers, capacity, width), lst).reshape(slots, width)
    arrived_ids = exchange(send_ids.reshape(peers, capacity), lst).reshape(slots)
    local = jnp.where(arrived_ids >= 0, arrived_ids - lax.axis_index(lst) * per_owner, -1)
    lookup = jnp.take(centroids, jnp.maximum(local, 0), axis=0)
    residual = jnp.where((local >= 0)[:, None], arrived.astype(F32) - lookup, 0.0).astype(BF16)
    member = (jnp.arange(per_owner, dtype=I32)[:, None] == local[None, :]).astype(BF16)
    sums = jnp.dot(member, residual, preferred_element_type=F32)
    counts = jnp.sum(member, axis=1, dtype=F32)
    total_sums = lax.psum(sums.astype(BF16), "grp").astype(F32)
    total_counts = prior_counts + lax.psum(counts, "grp")
    new_centroids = centroids + total_sums / total_counts[:, None]
    returned = exchange(residual.reshape(peers, capacity, width), lst).reshape(slots, width)
    return new_centroids, jnp.take(returned, where_to, axis=0)


def shards(new_rows, list_ids, rotation, centroids, prior_counts):
    groups, chips = lax.axis_size("grp"), lax.axis_size("chip")
    rows = new_rows.shape[0]
    per_owner = centroids.shape[0]
    capacity = max(8, 2 * rows // chips)
    me = lax.axis_index("grp").astype(I32).reshape(1)
    ids = list_ids.reshape(1, rows)
    ids = jnp.concatenate([ids] + [around(ids, "grp", k + 1) for k in range(groups - 1)], axis=0)
    place, spare, codes = assign(me, ids, chips, capacity, CORES * per_owner)
    codes = exchange(codes, ("chip", "core"))
    rotated, leaving = rotate(spare, new_rows, rotation)
    guests = [around(leaving[k * SPARE : (k + 1) * SPARE], "grp", k + 1) for k in range(3)]
    too_many = jnp.max(codes) >= FULL
    codes = codes.reshape(chips, CORES, capacity)
    return lax.cond(
        too_many,
        by_owner,
        by_chip,
        place,
        spare,
        codes,
        rotated,
        guests,
        list_ids,
        centroids,
        prior_counts,
    )


def solution(mesh):
    groups, owners = mesh.devices.shape
    parts = Mesh(mesh.devices.reshape(groups, owners // CORES, CORES), ("grp", "chip", "core"))
    every = ("grp", "chip", "core")
    lst = ("chip", "core")
    return jax.shard_map(
        shards,
        mesh=parts,
        in_specs=(P(every, None), P(every), P(), P(lst, None), P(lst)),
        out_specs=(P(lst, None), P(every, None)),
        check_vma=False,
    )
```

```python
import functools

import jax
import jax.numpy as jnp
from jax import lax
from jax.experimental import pallas as pl
from jax.experimental.pallas import tpu as pltpu
from jax.sharding import Mesh, PartitionSpec as P

CONTRACT_LAST = (((1,), (1,)), ((), ()))
CONTRACT_FIRST = (((0,), (0,)), ((), ()))
BF16 = jnp.bfloat16
F32 = jnp.float32
I32 = jnp.int32
CORES = 2
SPARE = 32
EXTRA = 128
FULL = 4096


def hot(mask):
    return jnp.where(mask, 1.0, 0.0).astype(BF16)


def iota(shape, dim):
    return lax.broadcasted_iota(I32, shape, dim)


def whole(shape):
    return pl.BlockSpec(shape, lambda *i: (0,) * len(shape))


def params():
    return pltpu.CompilerParams(vmem_limit_bytes=48 * 2**20)


def assign_kernel(groups, chips, capacity, per_chip, me_ref, ids_ref, place_ref, spare_ref, codes_ref):
    me = me_ref[0]
    rows = ids_ref.shape[1]
    earlier = hot(iota((rows, rows), 0) < iota((rows, rows), 1))
    cap = float(capacity)
    ids = [ids_ref[pl.ds(lax.rem(me - j + groups, groups), 1), :] for j in range(groups)]
    chip = [v // per_chip for v in ids]
    local = [v - c * per_chip + 1 for v, c in zip(ids, chip)]
    member = [iota((chips, rows), 0) == c for c in chip]
    member_f = [jnp.where(m, 1.0, 0.0) for m in member]
    before = jnp.dot(
        jnp.concatenate(member_f, axis=0).astype(BF16), earlier, preferred_element_type=F32
    )
    count = [jnp.sum(m, axis=1, keepdims=True) for m in member_f]
    free = [jnp.maximum(cap - n, 0.0) for n in count]
    over = [jnp.maximum(n - cap, 0.0) for n in count]
    free_at, over_at = [jnp.zeros_like(count[0])], [jnp.zeros_like(count[0])]
    for j in range(groups):
        free_at.append(free_at[-1] + free[j])
        over_at.append(over_at[-1] + over[j])
    lost = jnp.sum(jnp.maximum(over_at[-1] - free_at[-1], 0.0), axis=0, keepdims=True)
    target, slot = [], []
    for j in range(groups):
        rank = before[j * chips : (j + 1) * chips]
        stays = rank < cap
        entry = rank - cap + over_at[j]
        goes_to = jnp.full_like(rank, -1.0)
        lands = jnp.zeros_like(rank)
        for i in range(groups):
            inside = (entry >= free_at[i]) & (entry < free_at[i + 1])
            goes_to = jnp.where(inside, float(i), goes_to)
            lands = jnp.where(inside, count[i] + entry - free_at[i], lands)
        goes_to = jnp.where(stays, float(j), goes_to)
        lands = jnp.where(stays, rank, lands)
        target.append(jnp.sum(jnp.where(member[j], goes_to, 0.0), axis=0, keepdims=True).astype(I32))
        slot.append(jnp.sum(jnp.where(member[j], lands, 0.0), axis=0, keepdims=True).astype(I32))
    moves = [
        jnp.where(target[j] == i, 1.0, 0.0) if i != j else jnp.zeros((1, rows), F32)
        for j in range(groups)
        for i in range(groups)
    ]
    moves = jnp.concatenate(moves, axis=0)
    queue = jnp.dot(moves.astype(BF16), earlier, preferred_element_type=F32)
    totals = jnp.sum(moves, axis=1, keepdims=True)
    lost = lost + jnp.sum(jnp.maximum(totals - float(SPARE), 0.0), axis=0, keepdims=True)

    place = jnp.full((1, rows), -1, I32)
    spare = jnp.full((1, rows), -1, I32)
    arriving = jnp.zeros((8, EXTRA), F32)
    codes = jnp.zeros(codes_ref.shape, F32)
    for j in range(groups):
        mine = me == j
        flat = chip[j] * capacity + slot[j]
        place = jnp.where(mine & (target[j] == j), flat, place)
        for i in range(groups):
            if i == j:
                continue
            shift = (i - j) % groups - 1
            at = queue[j * groups + i : j * groups + i + 1].astype(I32) + shift * SPARE
            leaves = target[j] == i
            spare = jnp.where(mine & leaves, at, spare)
            to_me = hot((iota((EXTRA, rows), 0) == at) & leaves & (me == i))
            value = flat + 1
            high = value // 32
            low = value - high * 32
            pair = jnp.where(iota((8, rows), 0) == 0, high, low).astype(F32).astype(BF16)
            arriving = arriving + lax.dot_general(
                pair, to_me, CONTRACT_LAST, preferred_element_type=F32
            )
        at_slot = hot(iota((capacity, rows), 0) == slot[j])
        served = member[j] & (target[j] == me)
        high = local[j] // 32
        low = local[j] - high * 32
        for value, factor in ((high, 32.0), (low, 1.0)):
            spread = jnp.where(served, value.astype(F32), 0.0).astype(BF16)
            codes = codes + factor * lax.dot_general(
                spread, at_slot, CONTRACT_LAST, preferred_element_type=F32
            )
    place_ref[:, :rows] = place
    place_ref[:, rows:] = (arriving[0:1] * 32.0 + arriving[1:2]).astype(I32) - 1
    spare_ref[...] = spare
    codes_ref[...] = (codes + jnp.where(lost > 0.0, float(FULL), 0.0)).astype(I32)


def rotate_kernel(spare_ref, rows_ref, rotation_ref, rotated_ref, leaving_ref):
    rotated = jnp.dot(rows_ref[...], rotation_ref[...], preferred_element_type=F32).astype(BF16)
    rotated_ref[...] = rotated
    chosen = hot(iota((leaving_ref.shape[0], rotated.shape[0]), 0) == spare_ref[...])
    leaving_ref[...] = jnp.dot(chosen, rotated, preferred_element_type=F32).astype(BF16)


def pack_kernel(block, place_ref, rotated_ref, a_ref, b_ref, c_ref, send_ref, all_ref):
    step = pl.program_id(0)
    rows = rotated_ref.shape[0]

    @pl.when(step == 0)
    def _():
        all_ref[:rows] = rotated_ref[...]
        for k, ref in enumerate((a_ref, b_ref, c_ref)):
            all_ref[rows + k * SPARE : rows + (k + 1) * SPARE] = ref[...]
        all_ref[rows + 3 * SPARE :] = jnp.zeros((EXTRA - 3 * SPARE, all_ref.shape[1]), BF16)

    chosen = hot(iota((block, all_ref.shape[0]), 0) + step * block == place_ref[...])
    send_ref[...] = jnp.dot(chosen, all_ref[...], preferred_element_type=F32).astype(BF16)


def pick_kernel(place_ref, returned_ref, out_ref):
    chosen = hot(iota((returned_ref.shape[0], place_ref.shape[1]), 0) == place_ref[...])
    out_ref[...] = lax.dot_general(
        chosen, returned_ref[...], CONTRACT_FIRST, preferred_element_type=F32
    ).astype(BF16)


def join_kernel(spare_ref, own_ref, a_ref, b_ref, c_ref, out_ref):
    total = own_ref[...].astype(F32)
    spare = spare_ref[...]
    back = jnp.concatenate([a_ref[...], b_ref[...], c_ref[...]], axis=0)
    chosen = hot(iota((3 * SPARE, spare.shape[1]), 0) == spare)
    total = total + lax.dot_general(chosen, back, CONTRACT_FIRST, preferred_element_type=F32)
    out_ref[...] = total.astype(BF16)


def finish_kernel(me_ref, centroids_ref, *refs):
    out_ref = refs[-1]
    for k, ref in enumerate(refs[:-1]):

        @pl.when(pl.program_id(0) == k)
        def _(ref=ref):
            out_ref[...] = centroids_ref[...] + ref[...].astype(F32)


def shape(dims, dtype):
    return jax.ShapeDtypeStruct(dims, dtype)


def assign(me, ids, chips, capacity, per_chip):
    groups, rows = ids.shape
    return pl.pallas_call(
        functools.partial(assign_kernel, groups, chips, capacity, per_chip),
        in_specs=[pl.BlockSpec(memory_space=pltpu.SMEM), pl.BlockSpec(memory_space=pltpu.VMEM)],
        out_shape=(
            shape((1, rows + EXTRA), I32),
            shape((1, rows), I32),
            shape((chips, capacity), I32),
        ),
        compiler_params=params(),
        name="assign",
    )(me, ids)


def rotate(spare, new_rows, rotation):
    rows, width = new_rows.shape
    return pl.pallas_call(
        rotate_kernel,
        out_shape=(shape((rows, width), BF16), shape((EXTRA, width), BF16)),
        compiler_params=params(),
        name="rotate",
    )(spare, new_rows, rotation)


def pack(place, rotated, guests, slots):
    rows, width = rotated.shape
    block = 256
    return pl.pallas_call(
        functools.partial(pack_kernel, block),
        grid=(slots // block,),
        in_specs=[whole(place.shape), whole(rotated.shape)] + [whole(g.shape) for g in guests],
        out_specs=pl.BlockSpec((block, width), lambda i: (i, 0)),
        out_shape=shape((slots, width), BF16),
        scratch_shapes=[pltpu.VMEM((rows + EXTRA, width), BF16)],
        compiler_params=params(),
        name="pack",
    )(place, rotated, *guests)


def pick(place, returned):
    slots, width = returned.shape
    count = place.shape[1]
    block = 256
    return pl.pallas_call(
        pick_kernel,
        grid=(width // block,),
        in_specs=[whole(place.shape), pl.BlockSpec((slots, block), lambda i: (0, i))],
        out_specs=pl.BlockSpec((count, block), lambda i: (0, i)),
        out_shape=shape((count, width), BF16),
        compiler_params=params(),
        name="pick",
    )(place, returned)


def join(spare, own, guests):
    return pl.pallas_call(
        join_kernel,
        out_shape=shape(own.shape, BF16),
        compiler_params=params(),
        name="join",
    )(spare, own, *guests)


def finish(me, centroids, steps):
    groups = len(steps)
    quarter, width = steps[0].shape
    block = pl.BlockSpec((quarter, width), lambda k, me: (lax.rem(me[0] - k + groups, groups), 0))
    return pl.pallas_call(
        finish_kernel,
        grid_spec=pltpu.PrefetchScalarGridSpec(
            num_scalar_prefetch=1,
            grid=(groups,),
            in_specs=[block] + [whole(s.shape) for s in steps],
            out_specs=block,
        ),
        out_shape=shape(centroids.shape, F32),
        compiler_params=params(),
        name="finish",
    )(me, centroids, *steps)


def around(value, axis, shift):
    count = lax.axis_size(axis)
    return lax.ppermute(value, axis, [(i, (i + shift) % count) for i in range(count)])


def exchange(value, axes):
    return lax.all_to_all(value, axes, split_axis=0, concat_axis=0, tiled=True)


def by_chip(me, place, codes, far_codes, send, centroids, prior_counts):
    groups, chips = lax.axis_size("grp"), lax.axis_size("chip")
    core = lax.axis_index("core")
    per_owner, width = centroids.shape
    slots = send.shape[0]
    capacity = slots // chips
    arrived = exchange(send.reshape(chips, capacity, width), "chip").reshape(slots, width)
    table = jnp.concatenate([centroids, around(centroids, "core", 1)], axis=0)

    def nearness(codes):
        local = codes.reshape(slots) - 1
        near = local % per_owner
        near = jnp.where(local // per_owner == core, near, near + per_owner)
        return jnp.where(local >= 0, near, -1)

    here = nearness(codes)
    lookup = jnp.take(table, jnp.maximum(here, 0), axis=0)
    quarter = per_owner // groups
    lists = (jnp.arange(per_owner, dtype=I32) + me * quarter) % per_owner
    both = jnp.concatenate([here, nearness(far_codes)])
    counts = jnp.sum(lists[:, None] == both[None, :], axis=1, dtype=F32)
    counts = [
        around(counts[k * quarter : (k + 1) * quarter], "grp", k) if k else counts[:quarter]
        for k in range(groups)
    ]
    own_prior = lax.dynamic_slice_in_dim(prior_counts, me[0] * quarter, quarter)
    total_counts = own_prior + sum(counts[1:], counts[0])
    arrived, lookup, total_counts = lax.optimization_barrier((arrived, lookup, total_counts))
    residual = jnp.where((here >= 0)[:, None], arrived.astype(F32) - lookup, 0.0).astype(BF16)
    residual = lax.optimization_barrier(residual)
    returned = exchange(residual.reshape(chips, capacity, width), "chip").reshape(slots, width)
    far_sums = jnp.dot(
        (lists[:, None] + per_owner == here[None, :]).astype(BF16),
        residual,
        preferred_element_type=F32,
    ).astype(BF16)
    far_sums = around(far_sums, "core", 1)
    sums = jnp.dot(
        (lists[:, None] == here[None, :]).astype(BF16), residual, preferred_element_type=F32
    )
    sums = (sums + far_sums.astype(F32)).astype(BF16)
    parts = [
        around(sums[k * quarter : (k + 1) * quarter], "grp", k) if k else sums[:quarter]
        for k in range(groups)
    ]
    total = parts[0].astype(F32)
    for part in parts[1:]:
        total = total + part.astype(F32)
    step = (total / total_counts[:, None]).astype(BF16)
    steps = [step] + [around(step, "grp", k) for k in range(1, groups)]
    rows = place.shape[1] - EXTRA
    back = pick(place[:, rows:], returned)
    back = [around(back[k * SPARE : (k + 1) * SPARE], "grp", groups - k - 1) for k in range(3)]
    own = pick(place[:, :rows], returned)
    return steps, own, back


def by_owner(rotated, list_ids, centroids, prior_counts):
    lst = ("chip", "core")
    peers = lax.axis_size("chip") * CORES
    rows, width = rotated.shape
    per_owner = centroids.shape[0]
    capacity = max(2, 4 * rows // peers)
    slots = peers * capacity
    owner = list_ids // per_owner
    table = (owner[:, None] == jnp.arange(peers, dtype=I32)[None, :]).astype(I32)
    rank = jnp.sum(table * (jnp.cumsum(table, axis=0) - 1), axis=1)
    where_to = owner * capacity + rank
    source = jnp.full((slots,), rows, I32).at[where_to].set(jnp.arange(rows, dtype=I32))
    filled = source < rows
    safe = jnp.minimum(source, rows - 1)
    send = jnp.where(filled[:, None], jnp.take(rotated, safe, axis=0), jnp.zeros((), BF16))
    send_ids = jnp.where(filled, jnp.take(list_ids, safe, axis=0), -1)
    arrived = exchange(send.reshape(peers, capacity, width), lst).reshape(slots, width)
    arrived_ids = exchange(send_ids.reshape(peers, capacity), lst).reshape(slots)
    local = jnp.where(arrived_ids >= 0, arrived_ids - lax.axis_index(lst) * per_owner, -1)
    lookup = jnp.take(centroids, jnp.maximum(local, 0), axis=0)
    residual = jnp.where((local >= 0)[:, None], arrived.astype(F32) - lookup, 0.0).astype(BF16)
    member = (jnp.arange(per_owner, dtype=I32)[:, None] == local[None, :]).astype(BF16)
    sums = jnp.dot(member, residual, preferred_element_type=F32)
    counts = jnp.sum(member, axis=1, dtype=F32)
    total_sums = lax.psum(sums.astype(BF16), "grp").astype(F32)
    total_counts = prior_counts + lax.psum(counts, "grp")
    new_centroids = centroids + total_sums / total_counts[:, None]
    returned = exchange(residual.reshape(peers, capacity, width), lst).reshape(slots, width)
    return new_centroids, jnp.take(returned, where_to, axis=0)


def shards(new_rows, list_ids, rotation, centroids, prior_counts):
    groups, chips = lax.axis_size("grp"), lax.axis_size("chip")
    rows = new_rows.shape[0]
    per_owner = centroids.shape[0]
    capacity = max(8, 2 * rows // chips)
    me = lax.axis_index("grp").astype(I32).reshape(1)
    ids = list_ids.reshape(1, rows)
    ids = jnp.concatenate([ids] + [around(ids, "grp", k + 1) for k in range(groups - 1)], axis=0)
    place, spare, codes = assign(me, ids, chips, capacity, CORES * per_owner)
    codes = exchange(codes, "chip")
    rotated, leaving = rotate(spare, new_rows, rotation)
    guests = [around(leaving[k * SPARE : (k + 1) * SPARE], "grp", k + 1) for k in range(3)]
    send = pack(place, rotated, guests, chips * capacity)
    far_codes = around(codes, "core", 1)
    too_many = jnp.maximum(jnp.max(codes), jnp.max(far_codes)) >= FULL
    steps, own, back = by_chip(me, place, codes, far_codes, send, centroids, prior_counts)
    return lax.cond(
        too_many,
        lambda: by_owner(rotated, list_ids, centroids, prior_counts),
        lambda: (finish(me, centroids, steps), join(spare, own, back)),
    )


def solution(mesh):
    groups, owners = mesh.devices.shape
    parts = Mesh(mesh.devices.reshape(groups, owners // CORES, CORES), ("grp", "chip", "core"))
    every = ("grp", "chip", "core")
    lst = ("chip", "core")
    return jax.shard_map(
        shards,
        mesh=parts,
        in_specs=(P(every, None), P(every), P(), P(lst, None), P(lst)),
        out_specs=(P(lst, None), P(every, None)),
        check_vma=False,
    )
```

```python
import functools

import jax
import jax.numpy as jnp
from jax import lax
from jax.experimental import pallas as pl
from jax.experimental.pallas import tpu as pltpu
from jax.sharding import Mesh, PartitionSpec as P

CONTRACT_LAST = (((1,), (1,)), ((), ()))
CONTRACT_FIRST = (((0,), (0,)), ((), ()))
BF16 = jnp.bfloat16
F32 = jnp.float32
I32 = jnp.int32
CORES = 2
SPARE = 32
EXTRA = 128
FULL = 4096
LANES = 128
CUT = 384


def hot(mask):
    return jnp.where(mask, 1.0, 0.0).astype(BF16)


def iota(shape, dim):
    return lax.broadcasted_iota(I32, shape, dim)


def whole(shape):
    return pl.BlockSpec(shape, lambda *i: (0,) * len(shape))


def params():
    return pltpu.CompilerParams(vmem_limit_bytes=48 * 2**20)


def prepare_kernel(
    groups, chips, capacity, per_chip,
    me_ref, ids_ref, rows_hbm, rotation_hbm,
    place_ref, spare_ref, full_ref, first_ref, second_ref, a_ref, b_ref, c_ref,
    rows_ref, rotation_ref, sems,
):
    copies = [
        pltpu.make_async_copy(rows_hbm, rows_ref, sems.at[0]),
        pltpu.make_async_copy(rotation_hbm, rotation_ref, sems.at[1]),
    ]
    for copy in copies:
        copy.start()
    me = me_ref[0]
    rows = ids_ref.shape[1]
    earlier = hot(iota((rows, rows), 0) < iota((rows, rows), 1))
    cap = float(capacity)
    ids = [ids_ref[pl.ds(lax.rem(me - j + groups, groups), 1), :] for j in range(groups)]
    chip = [v // per_chip for v in ids]
    local = [v - c * per_chip + 1 for v, c in zip(ids, chip)]
    member = [iota((chips, rows), 0) == c for c in chip]
    member_f = [jnp.where(m, 1.0, 0.0) for m in member]
    before = jnp.dot(
        jnp.concatenate(member_f, axis=0).astype(BF16), earlier, preferred_element_type=F32
    )
    count = [jnp.sum(m, axis=1, keepdims=True) for m in member_f]
    free = [jnp.maximum(cap - n, 0.0) for n in count]
    over = [jnp.maximum(n - cap, 0.0) for n in count]
    free_at, over_at = [jnp.zeros_like(count[0])], [jnp.zeros_like(count[0])]
    for j in range(groups):
        free_at.append(free_at[-1] + free[j])
        over_at.append(over_at[-1] + over[j])
    lost = jnp.sum(jnp.maximum(over_at[-1] - free_at[-1], 0.0), axis=0, keepdims=True)
    target, slot = [], []
    for j in range(groups):
        rank = before[j * chips : (j + 1) * chips]
        stays = rank < cap
        entry = rank - cap + over_at[j]
        goes_to = jnp.full_like(rank, -1.0)
        lands = jnp.zeros_like(rank)
        for i in range(groups):
            inside = (entry >= free_at[i]) & (entry < free_at[i + 1])
            goes_to = jnp.where(inside, float(i), goes_to)
            lands = jnp.where(inside, count[i] + entry - free_at[i], lands)
        goes_to = jnp.where(stays, float(j), goes_to)
        lands = jnp.where(stays, rank, lands)
        target.append(jnp.sum(jnp.where(member[j], goes_to, 0.0), axis=0, keepdims=True).astype(I32))
        slot.append(jnp.sum(jnp.where(member[j], lands, 0.0), axis=0, keepdims=True).astype(I32))
    moves = [
        jnp.where(target[j] == i, 1.0, 0.0) if i != j else jnp.zeros((1, rows), F32)
        for j in range(groups)
        for i in range(groups)
    ]
    moves = jnp.concatenate(moves, axis=0)
    queue = jnp.dot(moves.astype(BF16), earlier, preferred_element_type=F32)
    totals = jnp.sum(moves, axis=1, keepdims=True)
    lost = lost + jnp.sum(jnp.maximum(totals - float(SPARE), 0.0), axis=0, keepdims=True)

    place = jnp.full((1, rows), -1, I32)
    spare = jnp.full((1, rows), -1, I32)
    arriving = jnp.zeros((8, EXTRA), F32)
    for j in range(groups):
        mine = me == j
        flat = chip[j] * capacity + slot[j]
        place = jnp.where(mine & (target[j] == j), flat, place)
        for i in range(groups):
            if i == j:
                continue
            shift = (i - j) % groups - 1
            at = queue[j * groups + i : j * groups + i + 1].astype(I32) + shift * SPARE
            leaves = target[j] == i
            spare = jnp.where(mine & leaves, at, spare)
            to_me = hot((iota((EXTRA, rows), 0) == at) & leaves & (me == i))
            value = flat + 1
            high = value // 32
            low = value - high * 32
            pair = jnp.where(iota((8, rows), 0) == 0, high, low).astype(F32).astype(BF16)
            arriving = arriving + lax.dot_general(
                pair, to_me, CONTRACT_LAST, preferred_element_type=F32
            )
    place_ref[:, :rows] = place
    place_ref[:, rows:] = (arriving[0:1] * 32.0 + arriving[1:2]).astype(I32) - 1
    spare_ref[...] = spare
    full_ref[...] = jnp.zeros(full_ref.shape, F32) + jnp.where(lost > 0.0, 1.0, 0.0)
    own = ids_ref[0:1, :]
    value = own - own // per_chip * per_chip + 1
    high = value // 32
    lane = iota((8, rows), 0)
    pair = jnp.where(lane == 0, high, jnp.where(lane == 1, value - high * 32, 0)).astype(F32)
    spread = hot(iota((8, LANES), 0) == iota((8, LANES), 1))
    first_ref[:, :LANES] = lax.dot_general(
        pair.astype(BF16), spread, CONTRACT_FIRST, preferred_element_type=F32
    ).astype(BF16)
    for copy in copies:
        copy.wait()
    rotated = jnp.dot(rows_ref[...], rotation_ref[...], preferred_element_type=F32).astype(BF16)
    first_ref[:, LANES:] = rotated[:, :CUT]
    second_ref[...] = rotated[:, CUT:]
    wide = first_ref.shape[1]
    for k, ref in enumerate((a_ref, b_ref, c_ref)):
        chosen = hot(iota((SPARE, rows), 0) + k * SPARE == spare)
        ref[:, :wide] = jnp.dot(chosen, first_ref[...], preferred_element_type=F32).astype(BF16)
        ref[:, wide:] = jnp.dot(chosen, second_ref[...], preferred_element_type=F32).astype(BF16)


def pack_kernel(block, offset, place_ref, full_ref, rows_ref, a_ref, b_ref, c_ref, send_ref, all_ref):
    step = pl.program_id(0)
    rows, wide = rows_ref.shape

    @pl.when(step == 0)
    def _():
        all_ref[:rows] = rows_ref[...]
        for k, ref in enumerate((a_ref, b_ref, c_ref)):
            all_ref[rows + k * SPARE : rows + (k + 1) * SPARE] = ref[:, offset : offset + wide]
        all_ref[rows + 3 * SPARE :] = jnp.zeros((EXTRA - 3 * SPARE, wide), BF16)

    chosen = hot(iota((block, all_ref.shape[0]), 0) + step * block == place_ref[...])
    packed = jnp.dot(chosen, all_ref[...], preferred_element_type=F32)
    if offset == 0:
        packed = packed + jnp.where(iota((block, wide), 1) == 2, full_ref[0:1, 0:1], 0.0)
    send_ref[...] = packed.astype(BF16)


def decode_kernel(arrived_ref, code_ref):
    take = hot(iota((8, LANES), 0) == iota((8, LANES), 1))
    parts = lax.dot_general(take, arrived_ref[...], CONTRACT_LAST, preferred_element_type=F32)
    code = parts[0:1] * 32.0 + parts[1:2] + parts[2:3] * float(FULL)
    code_ref[...] = code.astype(I32)


def filled(codes_ref):
    codes = codes_ref[...].astype(F32)
    return codes[:, 0:1] + codes[:, 1:2] > 0.0


def first_residual_kernel(arrived_ref, lookup_ref, out_ref):
    difference = arrived_ref[:, LANES:].astype(F32) - lookup_ref[...]
    out_ref[...] = jnp.where(filled(arrived_ref.at[:, :LANES]), difference, 0.0).astype(BF16)


def second_residual_kernel(codes_ref, arrived_ref, lookup_ref, first_ref, out_ref, second_ref):
    difference = arrived_ref[...].astype(F32) - lookup_ref[:, CUT:]
    second = jnp.where(filled(codes_ref), difference, 0.0).astype(BF16)
    out_ref[:, :CUT] = first_ref[...]
    out_ref[:, CUT:] = second
    second_ref[...] = second


def pick_kernel(place_ref, returned_ref, out_ref):
    chosen = hot(iota((returned_ref.shape[0], place_ref.shape[1]), 0) == place_ref[...])
    out_ref[...] = lax.dot_general(
        chosen, returned_ref[...], CONTRACT_FIRST, preferred_element_type=F32
    ).astype(BF16)


def join_kernel(spare_ref, own_ref, a_ref, b_ref, c_ref, out_ref):
    total = own_ref[...].astype(F32)
    spare = spare_ref[...]
    back = jnp.concatenate([a_ref[...], b_ref[...], c_ref[...]], axis=0)
    chosen = hot(iota((3 * SPARE, spare.shape[1]), 0) == spare)
    total = total + lax.dot_general(chosen, back, CONTRACT_FIRST, preferred_element_type=F32)
    out_ref[...] = total.astype(BF16)


def finish_kernel(me_ref, centroids_ref, *refs):
    out_ref = refs[-1]
    groups = len(refs) // 2
    for k in range(groups):

        @pl.when(pl.program_id(0) == k)
        def _(first=refs[k], second=refs[groups + k]):
            out_ref[:, :CUT] = centroids_ref[:, :CUT] + first[...].astype(F32)
            out_ref[:, CUT:] = centroids_ref[:, CUT:] + second[...].astype(F32)


def shape(dims, dtype):
    return jax.ShapeDtypeStruct(dims, dtype)


def prepare(me, ids, new_rows, rotation, chips, capacity, per_chip):
    groups, rows = ids.shape
    width = new_rows.shape[1]
    vmem, anywhere = pl.BlockSpec(memory_space=pltpu.VMEM), pl.BlockSpec(memory_space=pl.ANY)
    return pl.pallas_call(
        functools.partial(prepare_kernel, groups, chips, capacity, per_chip),
        in_specs=[pl.BlockSpec(memory_space=pltpu.SMEM), vmem, anywhere, anywhere],
        out_shape=(
            shape((1, rows + EXTRA), I32),
            shape((1, rows), I32),
            shape((1, LANES), F32),
            shape((rows, LANES + CUT), BF16),
            shape((rows, width - CUT), BF16),
        )
        + (shape((SPARE, LANES + width), BF16),) * 3,
        scratch_shapes=[
            pltpu.VMEM(new_rows.shape, BF16),
            pltpu.VMEM(rotation.shape, BF16),
            pltpu.SemaphoreType.DMA((2,)),
        ],
        compiler_params=params(),
        name="prepare",
    )(me, ids, new_rows, rotation)


def pack(place, full, rows, guests, offset, slots):
    count, wide = rows.shape
    block = 256
    return pl.pallas_call(
        functools.partial(pack_kernel, block, offset),
        grid=(slots // block,),
        in_specs=[whole(v.shape) for v in (place, full, rows, *guests)],
        out_specs=pl.BlockSpec((block, wide), lambda i: (i, 0)),
        out_shape=shape((slots, wide), BF16),
        scratch_shapes=[pltpu.VMEM((count + EXTRA, wide), BF16)],
        compiler_params=params(),
        name="pack",
    )(place, full, rows, *guests)


def decode(arrived):
    slots = arrived.shape[0]
    return pl.pallas_call(
        decode_kernel,
        grid=(1,),
        in_specs=[pl.BlockSpec((slots, LANES), lambda i: (0, 0))],
        out_specs=whole((1, slots)),
        out_shape=shape((1, slots), I32),
        compiler_params=params(),
        name="decode",
    )(arrived)


def first_residual(arrived, lookup):
    slots = arrived.shape[0]
    block = 256
    return pl.pallas_call(
        first_residual_kernel,
        grid=(slots // block,),
        in_specs=[
            pl.BlockSpec((block, LANES + CUT), lambda i: (i, 0)),
            pl.BlockSpec((block, CUT), lambda i: (i, 0)),
        ],
        out_specs=pl.BlockSpec((block, CUT), lambda i: (i, 0)),
        out_shape=shape((slots, CUT), BF16),
        compiler_params=params(),
        name="first_residual",
    )(arrived, lookup)


def second_residual(coded, arrived, lookup, first):
    slots, width = lookup.shape
    block = 256
    rest = width - CUT
    return pl.pallas_call(
        second_residual_kernel,
        grid=(slots // block,),
        in_specs=[
            pl.BlockSpec((block, LANES), lambda i: (i, 0)),
            pl.BlockSpec((block, rest), lambda i: (i, 0)),
            pl.BlockSpec((block, width), lambda i: (i, 0)),
            pl.BlockSpec((block, CUT), lambda i: (i, 0)),
        ],
        out_specs=(
            pl.BlockSpec((block, width), lambda i: (i, 0)),
            pl.BlockSpec((block, rest), lambda i: (i, 0)),
        ),
        out_shape=(shape((slots, width), BF16), shape((slots, rest), BF16)),
        compiler_params=params(),
        name="second_residual",
    )(coded, arrived, lookup, first)


def pick(place, returned):
    slots, width = returned.shape
    count = place.shape[1]
    block = 256
    return pl.pallas_call(
        pick_kernel,
        grid=(width // block,),
        in_specs=[whole(place.shape), pl.BlockSpec((slots, block), lambda i: (0, i))],
        out_specs=pl.BlockSpec((count, block), lambda i: (0, i)),
        out_shape=shape((count, width), BF16),
        compiler_params=params(),
        name="pick",
    )(place, returned)


def join(spare, own, guests):
    return pl.pallas_call(
        join_kernel,
        out_shape=shape(own.shape, BF16),
        compiler_params=params(),
        name="join",
    )(spare, own, *guests)


def finish(me, centroids, firsts, seconds):
    groups = len(firsts)
    quarter, width = firsts[0].shape[0], centroids.shape[1]
    block = pl.BlockSpec((quarter, width), lambda k, me: (lax.rem(me[0] - k + groups, groups), 0))
    return pl.pallas_call(
        finish_kernel,
        grid_spec=pltpu.PrefetchScalarGridSpec(
            num_scalar_prefetch=1,
            grid=(groups,),
            in_specs=[block] + [whole(s.shape) for s in (*firsts, *seconds)],
            out_specs=block,
        ),
        out_shape=shape(centroids.shape, F32),
        compiler_params=params(),
        name="finish",
    )(me, centroids, *firsts, *seconds)


def around(value, axis, shift):
    count = lax.axis_size(axis)
    return lax.ppermute(value, axis, [(i, (i + shift) % count) for i in range(count)])


def exchange(value, axes):
    return lax.all_to_all(value, axes, split_axis=0, concat_axis=0, tiled=True)


def quarters_around(value):
    groups = lax.axis_size("grp")
    quarter = value.shape[0] // groups
    return [value[:quarter]] + [
        around(value[k * quarter : (k + 1) * quarter], "grp", k) for k in range(1, groups)
    ]


def by_chip(me, place, full, first, second, guests, centroids, prior_counts):
    groups, chips = lax.axis_size("grp"), lax.axis_size("chip")
    core = lax.axis_index("core")
    per_owner, width = centroids.shape
    rows = first.shape[0]
    capacity = capacity_of(rows, chips)
    slots = chips * capacity
    quarter = per_owner // groups

    def to_chips(value):
        wide = value.shape[1]
        return exchange(value.reshape(chips, capacity, wide), "chip").reshape(slots, wide)

    coded = to_chips(pack(place, full, first, guests, 0, slots))
    arrived = to_chips(pack(place, full, second, guests, LANES + CUT, slots))
    code = decode(coded).reshape(slots)
    far_code = around(code, "core", 1)
    too_many = jnp.maximum(jnp.max(code), jnp.max(far_code)) >= FULL
    table = jnp.concatenate([centroids, around(centroids, "core", 1)], axis=0)

    def nearness(code):
        local = code - 1
        near = local % per_owner
        near = jnp.where(local // per_owner == core, near, near + per_owner)
        return jnp.where(local >= 0, near, -1)

    here = nearness(code)
    lookup = jnp.take(table, jnp.maximum(here, 0), axis=0, mode="clip")
    lists = (jnp.arange(per_owner, dtype=I32) + me * quarter) % per_owner
    both = jnp.concatenate([here, nearness(far_code)])
    counts = quarters_around(jnp.sum(lists[:, None] == both[None, :], axis=1, dtype=F32))
    own_prior = lax.dynamic_slice_in_dim(prior_counts, me[0] * quarter, quarter)
    total_counts = own_prior + sum(counts[1:], counts[0])

    def steps_of(residual):
        far = lists[:, None] + per_owner == here[None, :]
        far_sums = jnp.dot(far.astype(BF16), residual, preferred_element_type=F32).astype(BF16)
        far_sums = around(far_sums, "core", 1)
        near = lists[:, None] == here[None, :]
        sums = jnp.dot(near.astype(BF16), residual, preferred_element_type=F32)
        parts = quarters_around((sums + far_sums.astype(F32)).astype(BF16))
        total = parts[0].astype(F32)
        for part in parts[1:]:
            total = total + part.astype(F32)
        step = (total / total_counts[:, None]).astype(BF16)
        return [step] + [around(step, "grp", k) for k in range(1, groups)]

    first_part = first_residual(coded, lookup)
    residual, second_part = second_residual(coded, arrived, lookup, first_part)
    returned = to_chips(residual)
    new_centroids = finish(me, centroids, steps_of(first_part), steps_of(second_part))
    back = pick(place[:, rows:], returned)
    back = [around(back[k * SPARE : (k + 1) * SPARE], "grp", groups - k - 1) for k in range(3)]
    own = pick(place[:, :rows], returned)
    return too_many, new_centroids, own, back


def capacity_of(rows, chips):
    return max(8, 2 * rows // chips)


def by_owner(rotated, list_ids, centroids, prior_counts):
    lst = ("chip", "core")
    peers = lax.axis_size("chip") * CORES
    rows, width = rotated.shape
    per_owner = centroids.shape[0]
    capacity = max(2, 4 * rows // peers)
    slots = peers * capacity
    owner = list_ids // per_owner
    table = (owner[:, None] == jnp.arange(peers, dtype=I32)[None, :]).astype(I32)
    rank = jnp.sum(table * (jnp.cumsum(table, axis=0) - 1), axis=1)
    where_to = owner * capacity + rank
    source = jnp.full((slots,), rows, I32).at[where_to].set(jnp.arange(rows, dtype=I32))
    filled = source < rows
    safe = jnp.minimum(source, rows - 1)
    send = jnp.where(filled[:, None], jnp.take(rotated, safe, axis=0), jnp.zeros((), BF16))
    send_ids = jnp.where(filled, jnp.take(list_ids, safe, axis=0), -1)
    arrived = exchange(send.reshape(peers, capacity, width), lst).reshape(slots, width)
    arrived_ids = exchange(send_ids.reshape(peers, capacity), lst).reshape(slots)
    local = jnp.where(arrived_ids >= 0, arrived_ids - lax.axis_index(lst) * per_owner, -1)
    lookup = jnp.take(centroids, jnp.maximum(local, 0), axis=0)
    residual = jnp.where((local >= 0)[:, None], arrived.astype(F32) - lookup, 0.0).astype(BF16)
    member = (jnp.arange(per_owner, dtype=I32)[:, None] == local[None, :]).astype(BF16)
    sums = jnp.dot(member, residual, preferred_element_type=F32)
    counts = jnp.sum(member, axis=1, dtype=F32)
    total_sums = lax.psum(sums.astype(BF16), "grp").astype(F32)
    total_counts = prior_counts + lax.psum(counts, "grp")
    new_centroids = centroids + total_sums / total_counts[:, None]
    returned = exchange(residual.reshape(peers, capacity, width), lst).reshape(slots, width)
    return new_centroids, jnp.take(returned, where_to, axis=0)


def shards(new_rows, list_ids, rotation, centroids, prior_counts):
    groups, chips = lax.axis_size("grp"), lax.axis_size("chip")
    rows = new_rows.shape[0]
    per_chip = CORES * centroids.shape[0]
    me = lax.axis_index("grp").astype(I32).reshape(1)
    ids = list_ids.reshape(1, rows)
    ids = jnp.concatenate([ids] + [around(ids, "grp", k + 1) for k in range(groups - 1)], axis=0)
    place, spare, full, first, second, *leaving = prepare(
        me, ids, new_rows, rotation, chips, capacity_of(rows, chips), per_chip
    )
    guests = [around(v, "grp", k + 1) for k, v in enumerate(leaving)]
    too_many, new_centroids, own, back = by_chip(
        me, place, full, first, second, guests, centroids, prior_counts
    )

    def slow():
        rotated = jnp.concatenate([first[:, LANES:], second], axis=1)
        return by_owner(rotated, list_ids, centroids, prior_counts)

    return lax.cond(too_many, slow, lambda: (new_centroids, join(spare, own, back)))


def solution(mesh):
    groups, owners = mesh.devices.shape
    parts = Mesh(mesh.devices.reshape(groups, owners // CORES, CORES), ("grp", "chip", "core"))
    every = ("grp", "chip", "core")
    lst = ("chip", "core")
    return jax.shard_map(
        shards,
        mesh=parts,
        in_specs=(P(every, None), P(every), P(), P(lst, None), P(lst)),
        out_specs=(P(lst, None), P(every, None)),
        check_vma=False,
    )
```

```python
import functools

import jax
import jax.numpy as jnp
from jax import lax
from jax.experimental import pallas as pl
from jax.experimental.pallas import tpu as pltpu
from jax.sharding import Mesh, PartitionSpec as P

CONTRACT_LAST = (((1,), (1,)), ((), ()))
CONTRACT_FIRST = (((0,), (0,)), ((), ()))
BF16 = jnp.bfloat16
F32 = jnp.float32
I32 = jnp.int32
CORES = 2
SPARE = 32
EXTRA = 128
FULL = 4096


def hot(mask):
    return jnp.where(mask, 1.0, 0.0).astype(BF16)


def iota(shape, dim):
    return lax.broadcasted_iota(I32, shape, dim)


def whole(shape):
    return pl.BlockSpec(shape, lambda *i: (0,) * len(shape))


def params():
    return pltpu.CompilerParams(vmem_limit_bytes=48 * 2**20)


def assign_kernel(
    groups, chips, capacity, per_chip,
    me_ref, ids_ref, rows_ref, place_ref, spare_ref, codes_ref, *leaving_refs,
):
    me = me_ref[0]
    rows = ids_ref.shape[1]
    earlier = hot(iota((rows, rows), 0) < iota((rows, rows), 1))
    cap = float(capacity)
    ids = [ids_ref[pl.ds(lax.rem(me - j + groups, groups), 1), :] for j in range(groups)]
    chip = [v // per_chip for v in ids]
    local = [v - c * per_chip + 1 for v, c in zip(ids, chip)]
    member = [iota((chips, rows), 0) == c for c in chip]
    member_f = [jnp.where(m, 1.0, 0.0) for m in member]
    before = jnp.dot(
        jnp.concatenate(member_f, axis=0).astype(BF16), earlier, preferred_element_type=F32
    )
    count = [jnp.sum(m, axis=1, keepdims=True) for m in member_f]
    free = [jnp.maximum(cap - n, 0.0) for n in count]
    over = [jnp.maximum(n - cap, 0.0) for n in count]
    free_at, over_at = [jnp.zeros_like(count[0])], [jnp.zeros_like(count[0])]
    for j in range(groups):
        free_at.append(free_at[-1] + free[j])
        over_at.append(over_at[-1] + over[j])
    lost = jnp.sum(jnp.maximum(over_at[-1] - free_at[-1], 0.0), axis=0, keepdims=True)
    target, slot = [], []
    for j in range(groups):
        rank = before[j * chips : (j + 1) * chips]
        stays = rank < cap
        entry = rank - cap + over_at[j]
        goes_to = jnp.full_like(rank, -1.0)
        lands = jnp.zeros_like(rank)
        for i in range(groups):
            inside = (entry >= free_at[i]) & (entry < free_at[i + 1])
            goes_to = jnp.where(inside, float(i), goes_to)
            lands = jnp.where(inside, count[i] + entry - free_at[i], lands)
        goes_to = jnp.where(stays, float(j), goes_to)
        lands = jnp.where(stays, rank, lands)
        target.append(jnp.sum(jnp.where(member[j], goes_to, 0.0), axis=0, keepdims=True).astype(I32))
        slot.append(jnp.sum(jnp.where(member[j], lands, 0.0), axis=0, keepdims=True).astype(I32))
    moves = [
        jnp.where(target[j] == i, 1.0, 0.0) if i != j else jnp.zeros((1, rows), F32)
        for j in range(groups)
        for i in range(groups)
    ]
    moves = jnp.concatenate(moves, axis=0)
    queue = jnp.dot(moves.astype(BF16), earlier, preferred_element_type=F32)
    totals = jnp.sum(moves, axis=1, keepdims=True)
    lost = lost + jnp.sum(jnp.maximum(totals - float(SPARE), 0.0), axis=0, keepdims=True)

    place = jnp.full((1, rows), -1, I32)
    spare = jnp.full((1, rows), -1, I32)
    arriving = jnp.zeros((8, EXTRA), F32)
    codes = jnp.zeros(codes_ref.shape, F32)
    for j in range(groups):
        mine = me == j
        flat = chip[j] * capacity + slot[j]
        place = jnp.where(mine & (target[j] == j), flat, place)
        for i in range(groups):
            if i == j:
                continue
            shift = (i - j) % groups - 1
            at = queue[j * groups + i : j * groups + i + 1].astype(I32) + shift * SPARE
            leaves = target[j] == i
            spare = jnp.where(mine & leaves, at, spare)
            to_me = hot((iota((EXTRA, rows), 0) == at) & leaves & (me == i))
            value = flat + 1
            high = value // 32
            low = value - high * 32
            pair = jnp.where(iota((8, rows), 0) == 0, high, low).astype(F32).astype(BF16)
            arriving = arriving + lax.dot_general(
                pair, to_me, CONTRACT_LAST, preferred_element_type=F32
            )
        at_slot = hot(iota((capacity, rows), 0) == slot[j])
        served = member[j] & (target[j] == me)
        high = local[j] // 32
        low = local[j] - high * 32
        for value, factor in ((high, 32.0), (low, 1.0)):
            spread = jnp.where(served, value.astype(F32), 0.0).astype(BF16)
            codes = codes + factor * lax.dot_general(
                spread, at_slot, CONTRACT_LAST, preferred_element_type=F32
            )
    place_ref[:, :rows] = place
    place_ref[:, rows:] = (arriving[0:1] * 32.0 + arriving[1:2]).astype(I32) - 1
    spare_ref[...] = spare
    codes_ref[...] = (codes + jnp.where(lost > 0.0, float(FULL), 0.0)).astype(I32)
    for k, ref in enumerate(leaving_refs):
        chosen = hot(iota((SPARE, rows), 0) + k * SPARE == spare)
        ref[...] = jnp.dot(chosen, rows_ref[...], preferred_element_type=F32).astype(BF16)


def pack_kernel(block, place_ref, rows_ref, rotation_ref, a_ref, b_ref, c_ref, send_ref, all_ref):
    step = pl.program_id(0)
    rows = rows_ref.shape[0]

    @pl.when(step == 0)
    def _():
        def rotate(value):
            return jnp.dot(value, rotation_ref[...], preferred_element_type=F32).astype(BF16)

        guests = jnp.concatenate([a_ref[...], b_ref[...], c_ref[...]], axis=0)
        all_ref[:rows] = rotate(rows_ref[...])
        all_ref[rows : rows + 3 * SPARE] = rotate(guests)
        all_ref[rows + 3 * SPARE :] = jnp.zeros((EXTRA - 3 * SPARE, all_ref.shape[1]), BF16)

    chosen = hot(iota((block, all_ref.shape[0]), 0) + step * block == place_ref[...])
    send_ref[...] = jnp.dot(chosen, all_ref[...], preferred_element_type=F32).astype(BF16)


def pick_kernel(place_ref, returned_ref, out_ref):
    chosen = hot(iota((returned_ref.shape[0], place_ref.shape[1]), 0) == place_ref[...])
    out_ref[...] = lax.dot_general(
        chosen, returned_ref[...], CONTRACT_FIRST, preferred_element_type=F32
    ).astype(BF16)


def join_kernel(spare_ref, own_ref, a_ref, b_ref, c_ref, out_ref):
    total = own_ref[...].astype(F32)
    spare = spare_ref[...]
    back = jnp.concatenate([a_ref[...], b_ref[...], c_ref[...]], axis=0)
    chosen = hot(iota((3 * SPARE, spare.shape[1]), 0) == spare)
    total = total + lax.dot_general(chosen, back, CONTRACT_FIRST, preferred_element_type=F32)
    out_ref[...] = total.astype(BF16)


def finish_kernel(me_ref, *refs):
    centroids_ref, step_ref, out_ref = refs[-3:]
    out_ref[...] = centroids_ref[...] + step_ref[...].astype(F32)


def shape(dims, dtype):
    return jax.ShapeDtypeStruct(dims, dtype)


def assign(me, ids, new_rows, chips, capacity, per_chip):
    groups, rows = ids.shape
    vmem = pl.BlockSpec(memory_space=pltpu.VMEM)
    return pl.pallas_call(
        functools.partial(assign_kernel, groups, chips, capacity, per_chip),
        in_specs=[pl.BlockSpec(memory_space=pltpu.SMEM), vmem, vmem],
        out_shape=(
            shape((1, rows + EXTRA), I32),
            shape((1, rows), I32),
            shape((chips, capacity), I32),
        )
        + (shape((SPARE, new_rows.shape[1]), BF16),) * 3,
        compiler_params=params(),
        name="assign",
    )(me, ids, new_rows)


def pack(place, new_rows, rotation, guests, slots):
    rows, width = new_rows.shape
    block = 256
    return pl.pallas_call(
        functools.partial(pack_kernel, block),
        grid=(slots // block,),
        in_specs=[whole(v.shape) for v in (place, new_rows, rotation, *guests)],
        out_specs=pl.BlockSpec((block, width), lambda i: (i, 0)),
        out_shape=shape((slots, width), BF16),
        scratch_shapes=[pltpu.VMEM((rows + EXTRA, width), BF16)],
        compiler_params=params(),
        name="pack",
    )(place, new_rows, rotation, *guests)


def pick(place, returned):
    slots, width = returned.shape
    count = place.shape[1]
    block = 256
    return pl.pallas_call(
        pick_kernel,
        grid=(width // block,),
        in_specs=[whole(place.shape), pl.BlockSpec((slots, block), lambda i: (0, i))],
        out_specs=pl.BlockSpec((count, block), lambda i: (0, i)),
        out_shape=shape((count, width), BF16),
        compiler_params=params(),
        name="pick",
    )(place, returned)


def join(spare, own, guests):
    return pl.pallas_call(
        join_kernel,
        out_shape=shape(own.shape, BF16),
        compiler_params=params(),
        name="join",
    )(spare, own, *guests)


def finish(me, centroids, steps):
    groups = len(steps)
    quarter, width = steps[0].shape
    made = ()
    for k, step in enumerate(steps):
        block = pl.BlockSpec(
            (quarter, width), lambda i, me, k=k: (lax.rem(me[0] - k + groups, groups), 0)
        )
        out = pl.pallas_call(
            finish_kernel,
            grid_spec=pltpu.PrefetchScalarGridSpec(
                num_scalar_prefetch=1,
                grid=(1,),
                in_specs=[pl.BlockSpec(memory_space=pl.ANY)] * len(made)
                + [block, whole(step.shape)],
                out_specs=block,
            ),
            out_shape=shape(centroids.shape, F32),
            input_output_aliases={1: 0} if made else {},
            compiler_params=params(),
            name="finish",
        )(me, *made, centroids, step)
        made = (out,)
    return out


def around(value, axis, shift):
    count = lax.axis_size(axis)
    return lax.ppermute(value, axis, [(i, (i + shift) % count) for i in range(count)])


def exchange(value, axes):
    return lax.all_to_all(value, axes, split_axis=0, concat_axis=0, tiled=True)


def by_chip(me, place, codes, far_codes, send, centroids, prior_counts):
    groups, chips = lax.axis_size("grp"), lax.axis_size("chip")
    core = lax.axis_index("core")
    per_owner, width = centroids.shape
    slots = send.shape[0]
    capacity = slots // chips
    arrived = exchange(send.reshape(chips, capacity, width), "chip").reshape(slots, width)
    table = jnp.concatenate([centroids, around(centroids, "core", 1)], axis=0)

    def nearness(codes):
        local = codes.reshape(slots) - 1
        near = local % per_owner
        near = jnp.where(local // per_owner == core, near, near + per_owner)
        return jnp.where(local >= 0, near, -1)

    here = nearness(codes)
    lookup = jnp.take(table, jnp.maximum(here, 0), axis=0, mode="clip")
    quarter = per_owner // groups
    lists = (jnp.arange(per_owner, dtype=I32) + me * quarter) % per_owner
    both = jnp.concatenate([here, nearness(far_codes)])
    counts = jnp.sum(lists[:, None] == both[None, :], axis=1, dtype=F32)
    counts = [
        around(counts[k * quarter : (k + 1) * quarter], "grp", k) if k else counts[:quarter]
        for k in range(groups)
    ]
    own_prior = lax.dynamic_slice_in_dim(prior_counts, me[0] * quarter, quarter)
    total_counts = own_prior + sum(counts[1:], counts[0])
    arrived, lookup, total_counts = lax.optimization_barrier((arrived, lookup, total_counts))
    residual = lax.optimization_barrier((arrived.astype(F32) - lookup).astype(BF16))
    returned = exchange(residual.reshape(chips, capacity, width), "chip").reshape(slots, width)
    far_sums = jnp.dot(
        (lists[:, None] + per_owner == here[None, :]).astype(BF16),
        residual,
        preferred_element_type=F32,
    ).astype(BF16)
    far_sums = around(far_sums, "core", 1)
    sums = jnp.dot(
        (lists[:, None] == here[None, :]).astype(BF16), residual, preferred_element_type=F32
    )
    sums = (sums + far_sums.astype(F32)).astype(BF16)
    parts = [
        around(sums[k * quarter : (k + 1) * quarter], "grp", k) if k else sums[:quarter]
        for k in range(groups)
    ]
    total = parts[0].astype(F32)
    for part in parts[1:]:
        total = total + part.astype(F32)
    step = (total / total_counts[:, None]).astype(BF16)
    steps = [step] + [around(step, "grp", k) for k in range(1, groups)]
    rows = place.shape[1] - EXTRA
    back = pick(place[:, rows:], returned)
    back = [around(back[k * SPARE : (k + 1) * SPARE], "grp", groups - k - 1) for k in range(3)]
    own = pick(place[:, :rows], returned)
    steps[-1], own = lax.optimization_barrier((steps[-1], own))
    new_centroids = finish(me, centroids, steps)
    return new_centroids, own, back


def by_owner(rotated, list_ids, centroids, prior_counts):
    lst = ("chip", "core")
    peers = lax.axis_size("chip") * CORES
    rows, width = rotated.shape
    per_owner = centroids.shape[0]
    capacity = max(2, 4 * rows // peers)
    slots = peers * capacity
    owner = list_ids // per_owner
    table = (owner[:, None] == jnp.arange(peers, dtype=I32)[None, :]).astype(I32)
    rank = jnp.sum(table * (jnp.cumsum(table, axis=0) - 1), axis=1)
    where_to = owner * capacity + rank
    source = jnp.full((slots,), rows, I32).at[where_to].set(jnp.arange(rows, dtype=I32))
    filled = source < rows
    safe = jnp.minimum(source, rows - 1)
    send = jnp.where(filled[:, None], jnp.take(rotated, safe, axis=0), jnp.zeros((), BF16))
    send_ids = jnp.where(filled, jnp.take(list_ids, safe, axis=0), -1)
    arrived = exchange(send.reshape(peers, capacity, width), lst).reshape(slots, width)
    arrived_ids = exchange(send_ids.reshape(peers, capacity), lst).reshape(slots)
    local = jnp.where(arrived_ids >= 0, arrived_ids - lax.axis_index(lst) * per_owner, -1)
    lookup = jnp.take(centroids, jnp.maximum(local, 0), axis=0)
    residual = jnp.where((local >= 0)[:, None], arrived.astype(F32) - lookup, 0.0).astype(BF16)
    member = (jnp.arange(per_owner, dtype=I32)[:, None] == local[None, :]).astype(BF16)
    sums = jnp.dot(member, residual, preferred_element_type=F32)
    counts = jnp.sum(member, axis=1, dtype=F32)
    total_sums = lax.psum(sums.astype(BF16), "grp").astype(F32)
    total_counts = prior_counts + lax.psum(counts, "grp")
    new_centroids = centroids + total_sums / total_counts[:, None]
    returned = exchange(residual.reshape(peers, capacity, width), lst).reshape(slots, width)
    return new_centroids, jnp.take(returned, where_to, axis=0)


def shards(new_rows, list_ids, rotation, centroids, prior_counts):
    groups, chips = lax.axis_size("grp"), lax.axis_size("chip")
    rows = new_rows.shape[0]
    per_owner = centroids.shape[0]
    capacity = max(8, 2 * rows // chips)
    me = lax.axis_index("grp").astype(I32).reshape(1)
    ids = list_ids.reshape(1, rows)
    ids = jnp.concatenate([ids] + [around(ids, "grp", k + 1) for k in range(groups - 1)], axis=0)
    place, spare, codes, *leaving = assign(
        me, ids, new_rows, chips, capacity, CORES * per_owner
    )
    codes = exchange(codes, "chip")
    guests = [around(v, "grp", k + 1) for k, v in enumerate(leaving)]
    send = pack(place, new_rows, rotation, guests, chips * capacity)
    far_codes = around(codes, "core", 1)
    too_many = jnp.maximum(jnp.max(codes), jnp.max(far_codes)) >= FULL
    new_centroids, own, back = by_chip(me, place, codes, far_codes, send, centroids, prior_counts)

    def slow():
        rotated = jnp.dot(new_rows, rotation, preferred_element_type=F32).astype(BF16)
        return by_owner(rotated, list_ids, centroids, prior_counts)

    return lax.cond(too_many, slow, lambda: (new_centroids, join(spare, own, back)))


def solution(mesh):
    groups, owners = mesh.devices.shape
    parts = Mesh(mesh.devices.reshape(groups, owners // CORES, CORES), ("grp", "chip", "core"))
    every = ("grp", "chip", "core")
    lst = ("chip", "core")
    return jax.shard_map(
        shards,
        mesh=parts,
        in_specs=(P(every, None), P(every), P(), P(lst, None), P(lst)),
        out_specs=(P(lst, None), P(every, None)),
        check_vma=False,
    )
```

```python
import functools

import jax
import jax.numpy as jnp
from jax import lax
from jax.experimental import pallas as pl
from jax.experimental.pallas import tpu as pltpu
from jax.sharding import Mesh, PartitionSpec as P

CONTRACT_LAST = (((1,), (1,)), ((), ()))
CONTRACT_FIRST = (((0,), (0,)), ((), ()))
BF16 = jnp.bfloat16
F32 = jnp.float32
I32 = jnp.int32
CORES = 2
SPARE = 32
EXTRA = 128
FULL = 4096


def hot(mask):
    return jnp.where(mask, 1.0, 0.0).astype(BF16)


def iota(shape, dim):
    return lax.broadcasted_iota(I32, shape, dim)


def whole(shape):
    return pl.BlockSpec(shape, lambda *i: (0,) * len(shape))


def params():
    return pltpu.CompilerParams(vmem_limit_bytes=48 * 2**20)


def assign_kernel(
    groups, chips, capacity, per_chip,
    me_ref, ids_ref, rows_ref, place_ref, spare_ref, codes_ref, *leaving_refs,
):
    me = me_ref[0]
    rows = ids_ref.shape[1]
    earlier = hot(iota((rows, rows), 0) < iota((rows, rows), 1))
    cap = float(capacity)
    ids = [ids_ref[pl.ds(lax.rem(me - j + groups, groups), 1), :] for j in range(groups)]
    chip = [v // per_chip for v in ids]
    local = [v - c * per_chip + 1 for v, c in zip(ids, chip)]
    member = [iota((chips, rows), 0) == c for c in chip]
    member_f = [jnp.where(m, 1.0, 0.0) for m in member]
    before = jnp.dot(
        jnp.concatenate(member_f, axis=0).astype(BF16), earlier, preferred_element_type=F32
    )
    count = [jnp.sum(m, axis=1, keepdims=True) for m in member_f]
    free = [jnp.maximum(cap - n, 0.0) for n in count]
    over = [jnp.maximum(n - cap, 0.0) for n in count]
    free_at, over_at = [jnp.zeros_like(count[0])], [jnp.zeros_like(count[0])]
    for j in range(groups):
        free_at.append(free_at[-1] + free[j])
        over_at.append(over_at[-1] + over[j])
    lost = jnp.sum(jnp.maximum(over_at[-1] - free_at[-1], 0.0), axis=0, keepdims=True)
    target, slot = [], []
    for j in range(groups):
        rank = before[j * chips : (j + 1) * chips]
        stays = rank < cap
        entry = rank - cap + over_at[j]
        goes_to = jnp.full_like(rank, -1.0)
        lands = jnp.zeros_like(rank)
        for i in range(groups):
            inside = (entry >= free_at[i]) & (entry < free_at[i + 1])
            goes_to = jnp.where(inside, float(i), goes_to)
            lands = jnp.where(inside, count[i] + entry - free_at[i], lands)
        goes_to = jnp.where(stays, float(j), goes_to)
        lands = jnp.where(stays, rank, lands)
        target.append(jnp.sum(jnp.where(member[j], goes_to, 0.0), axis=0, keepdims=True).astype(I32))
        slot.append(jnp.sum(jnp.where(member[j], lands, 0.0), axis=0, keepdims=True).astype(I32))
    moves = [
        jnp.where(target[j] == i, 1.0, 0.0) if i != j else jnp.zeros((1, rows), F32)
        for j in range(groups)
        for i in range(groups)
    ]
    moves = jnp.concatenate(moves, axis=0)
    queue = jnp.dot(moves.astype(BF16), earlier, preferred_element_type=F32)
    totals = jnp.sum(moves, axis=1, keepdims=True)
    lost = lost + jnp.sum(jnp.maximum(totals - float(SPARE), 0.0), axis=0, keepdims=True)

    place = jnp.full((1, rows), -1, I32)
    spare = jnp.full((1, rows), -1, I32)
    arriving = jnp.zeros((8, EXTRA), F32)
    codes = jnp.zeros(codes_ref.shape, F32)
    for j in range(groups):
        mine = me == j
        flat = chip[j] * capacity + slot[j]
        place = jnp.where(mine & (target[j] == j), flat, place)
        for i in range(groups):
            if i == j:
                continue
            shift = (i - j) % groups - 1
            at = queue[j * groups + i : j * groups + i + 1].astype(I32) + shift * SPARE
            leaves = target[j] == i
            spare = jnp.where(mine & leaves, at, spare)
            to_me = hot((iota((EXTRA, rows), 0) == at) & leaves & (me == i))
            value = flat + 1
            high = value // 32
            low = value - high * 32
            pair = jnp.where(iota((8, rows), 0) == 0, high, low).astype(F32).astype(BF16)
            arriving = arriving + lax.dot_general(
                pair, to_me, CONTRACT_LAST, preferred_element_type=F32
            )
        at_slot = hot(iota((capacity, rows), 0) == slot[j])
        served = member[j] & (target[j] == me)
        high = local[j] // 32
        low = local[j] - high * 32
        for value, factor in ((high, 32.0), (low, 1.0)):
            spread = jnp.where(served, value.astype(F32), 0.0).astype(BF16)
            codes = codes + factor * lax.dot_general(
                spread, at_slot, CONTRACT_LAST, preferred_element_type=F32
            )
    place_ref[:, :rows] = place
    place_ref[:, rows:] = (arriving[0:1] * 32.0 + arriving[1:2]).astype(I32) - 1
    spare_ref[...] = spare
    codes_ref[...] = (codes + jnp.where(lost > 0.0, float(FULL), 0.0)).astype(I32)
    for k, ref in enumerate(leaving_refs):
        chosen = hot(iota((SPARE, rows), 0) + k * SPARE == spare)
        ref[...] = jnp.dot(chosen, rows_ref[...], preferred_element_type=F32).astype(BF16)


def pack_kernel(block, place_ref, rows_ref, rotation_ref, a_ref, b_ref, c_ref, send_ref, all_ref):
    step = pl.program_id(0)
    rows = rows_ref.shape[0]

    @pl.when(step == 0)
    def _():
        def rotate(value):
            return jnp.dot(value, rotation_ref[...], preferred_element_type=F32).astype(BF16)

        guests = jnp.concatenate([a_ref[...], b_ref[...], c_ref[...]], axis=0)
        all_ref[:rows] = rotate(rows_ref[...])
        all_ref[rows : rows + 3 * SPARE] = rotate(guests)
        all_ref[rows + 3 * SPARE :] = jnp.zeros((EXTRA - 3 * SPARE, all_ref.shape[1]), BF16)

    chosen = hot(iota((block, all_ref.shape[0]), 0) + step * block == place_ref[...])
    send_ref[...] = jnp.dot(chosen, all_ref[...], preferred_element_type=F32).astype(BF16)


def pick_kernel(place_ref, returned_ref, own_ref, a_ref, b_ref, c_ref, chosen_ref):
    rows = own_ref.shape[0]

    @pl.when(pl.program_id(0) == 0)
    def _():
        chosen_ref[...] = hot(iota(chosen_ref.shape, 0) == place_ref[...])

    picked = lax.dot_general(
        chosen_ref[...], returned_ref[...], CONTRACT_FIRST, preferred_element_type=F32
    ).astype(BF16)
    own_ref[...] = picked[:rows]
    for k, ref in enumerate((a_ref, b_ref, c_ref)):
        ref[...] = picked[rows + k * SPARE : rows + (k + 1) * SPARE]


def join_kernel(spare_ref, own_ref, a_ref, b_ref, c_ref, out_ref):
    total = own_ref[...].astype(F32)
    spare = spare_ref[...]
    back = jnp.concatenate([a_ref[...], b_ref[...], c_ref[...]], axis=0)
    chosen = hot(iota((3 * SPARE, spare.shape[1]), 0) == spare)
    total = total + lax.dot_general(chosen, back, CONTRACT_FIRST, preferred_element_type=F32)
    out_ref[...] = total.astype(BF16)


def finish_kernel(me_ref, *refs):
    centroids_ref, step_ref, out_ref = refs[-3:]
    out_ref[...] = centroids_ref[...] + step_ref[...].astype(F32)


def shape(dims, dtype):
    return jax.ShapeDtypeStruct(dims, dtype)


def assign(me, ids, new_rows, chips, capacity, per_chip):
    groups, rows = ids.shape
    vmem = pl.BlockSpec(memory_space=pltpu.VMEM)
    return pl.pallas_call(
        functools.partial(assign_kernel, groups, chips, capacity, per_chip),
        in_specs=[pl.BlockSpec(memory_space=pltpu.SMEM), vmem, vmem],
        out_shape=(
            shape((1, rows + EXTRA), I32),
            shape((1, rows), I32),
            shape((chips, capacity), I32),
        )
        + (shape((SPARE, new_rows.shape[1]), BF16),) * 3,
        compiler_params=params(),
        name="assign",
    )(me, ids, new_rows)


def pack(place, new_rows, rotation, guests, slots):
    rows, width = new_rows.shape
    block = 256
    return pl.pallas_call(
        functools.partial(pack_kernel, block),
        grid=(slots // block,),
        in_specs=[whole(v.shape) for v in (place, new_rows, rotation, *guests)],
        out_specs=pl.BlockSpec((block, width), lambda i: (i, 0)),
        out_shape=shape((slots, width), BF16),
        scratch_shapes=[pltpu.VMEM((rows + EXTRA, width), BF16)],
        compiler_params=params(),
        name="pack",
    )(place, new_rows, rotation, *guests)


def pick(place, returned):
    slots, width = returned.shape
    rows = place.shape[1] - EXTRA
    block = 256

    def columns(count):
        return pl.BlockSpec((count, block), lambda i: (0, i))

    return pl.pallas_call(
        pick_kernel,
        grid=(width // block,),
        in_specs=[whole(place.shape), columns(slots)],
        out_specs=(columns(rows),) + (columns(SPARE),) * 3,
        out_shape=(shape((rows, width), BF16),) + (shape((SPARE, width), BF16),) * 3,
        scratch_shapes=[pltpu.VMEM((slots, place.shape[1]), BF16)],
        compiler_params=params(),
        name="pick",
    )(place, returned)


def join(spare, own, guests):
    return pl.pallas_call(
        join_kernel,
        out_shape=shape(own.shape, BF16),
        compiler_params=params(),
        name="join",
    )(spare, own, *guests)


def finish(me, made, centroids, step, shift):
    groups = lax.axis_size("grp")
    block = pl.BlockSpec(step.shape, lambda i, me: (lax.rem(me[0] - shift + groups, groups), 0))
    return pl.pallas_call(
        finish_kernel,
        grid_spec=pltpu.PrefetchScalarGridSpec(
            num_scalar_prefetch=1,
            grid=(1,),
            in_specs=[pl.BlockSpec(memory_space=pl.ANY)] * len(made) + [block, whole(step.shape)],
            out_specs=block,
        ),
        out_shape=pltpu.HBM(centroids.shape, F32),
        input_output_aliases={1: 0} if made else {},
        compiler_params=params(),
        name="finish",
    )(me, *made, centroids, step)


def around(value, axis, shift):
    count = lax.axis_size(axis)
    return lax.ppermute(value, axis, [(i, (i + shift) % count) for i in range(count)])


def exchange(value, axes):
    return lax.all_to_all(value, axes, split_axis=0, concat_axis=0, tiled=True)


def by_chip(me, place, codes, far_codes, send, centroids, prior_counts):
    groups, chips = lax.axis_size("grp"), lax.axis_size("chip")
    core = lax.axis_index("core")
    per_owner, width = centroids.shape
    slots = send.shape[0]
    capacity = slots // chips
    arrived = exchange(send.reshape(chips, capacity, width), "chip").reshape(slots, width)
    table = jnp.concatenate([centroids, around(centroids, "core", 1)], axis=0)

    def nearness(codes):
        local = codes.reshape(slots) - 1
        near = local % per_owner
        near = jnp.where(local // per_owner == core, near, near + per_owner)
        return jnp.where(local >= 0, near, -1)

    here = nearness(codes)
    lookup = jnp.take(table, jnp.maximum(here, 0), axis=0, mode="clip")
    quarter = per_owner // groups
    lists = (jnp.arange(per_owner, dtype=I32) + me * quarter) % per_owner
    both = jnp.concatenate([here, nearness(far_codes)])
    counts = jnp.sum(lists[:, None] == both[None, :], axis=1, dtype=F32)
    counts = [
        around(counts[k * quarter : (k + 1) * quarter], "grp", k) if k else counts[:quarter]
        for k in range(groups)
    ]
    own_prior = lax.dynamic_slice_in_dim(prior_counts, me[0] * quarter, quarter)
    total_counts = own_prior + sum(counts[1:], counts[0])
    arrived, lookup, total_counts = lax.optimization_barrier((arrived, lookup, total_counts))
    residual = lax.optimization_barrier((arrived.astype(F32) - lookup).astype(BF16))
    returned = exchange(residual.reshape(chips, capacity, width), "chip").reshape(slots, width)
    far_sums = jnp.dot(
        (lists[:, None] + per_owner == here[None, :]).astype(BF16),
        residual,
        preferred_element_type=F32,
    ).astype(BF16)
    far_sums = around(far_sums, "core", 1)
    sums = jnp.dot(
        (lists[:, None] == here[None, :]).astype(BF16), residual, preferred_element_type=F32
    )
    sums = (sums + far_sums.astype(F32)).astype(BF16)
    parts = [
        around(sums[k * quarter : (k + 1) * quarter], "grp", k) if k else sums[:quarter]
        for k in range(groups)
    ]
    total = parts[0].astype(F32)
    for part in parts[1:]:
        total = total + part.astype(F32)
    step = (total / total_counts[:, None]).astype(BF16)
    others = [around(step, "grp", k) for k in range(1, groups)]
    new_centroids = finish(me, (), centroids, step, 0)
    returned, new_centroids = lax.optimization_barrier((returned, new_centroids))
    own, *back = pick(place, returned)
    back = [around(v, "grp", groups - k - 1) for k, v in enumerate(back)]
    for k in range(1, groups):
        new_centroids = finish(me, (new_centroids,), centroids, others[k - 1], k)
    return new_centroids, own, back


def by_owner(rotated, list_ids, centroids, prior_counts):
    lst = ("chip", "core")
    peers = lax.axis_size("chip") * CORES
    rows, width = rotated.shape
    per_owner = centroids.shape[0]
    capacity = max(2, 4 * rows // peers)
    slots = peers * capacity
    owner = list_ids // per_owner
    table = (owner[:, None] == jnp.arange(peers, dtype=I32)[None, :]).astype(I32)
    rank = jnp.sum(table * (jnp.cumsum(table, axis=0) - 1), axis=1)
    where_to = owner * capacity + rank
    source = jnp.full((slots,), rows, I32).at[where_to].set(jnp.arange(rows, dtype=I32))
    filled = source < rows
    safe = jnp.minimum(source, rows - 1)
    send = jnp.where(filled[:, None], jnp.take(rotated, safe, axis=0), jnp.zeros((), BF16))
    send_ids = jnp.where(filled, jnp.take(list_ids, safe, axis=0), -1)
    arrived = exchange(send.reshape(peers, capacity, width), lst).reshape(slots, width)
    arrived_ids = exchange(send_ids.reshape(peers, capacity), lst).reshape(slots)
    local = jnp.where(arrived_ids >= 0, arrived_ids - lax.axis_index(lst) * per_owner, -1)
    lookup = jnp.take(centroids, jnp.maximum(local, 0), axis=0)
    residual = jnp.where((local >= 0)[:, None], arrived.astype(F32) - lookup, 0.0).astype(BF16)
    member = (jnp.arange(per_owner, dtype=I32)[:, None] == local[None, :]).astype(BF16)
    sums = jnp.dot(member, residual, preferred_element_type=F32)
    counts = jnp.sum(member, axis=1, dtype=F32)
    total_sums = lax.psum(sums.astype(BF16), "grp").astype(F32)
    total_counts = prior_counts + lax.psum(counts, "grp")
    new_centroids = centroids + total_sums / total_counts[:, None]
    returned = exchange(residual.reshape(peers, capacity, width), lst).reshape(slots, width)
    return new_centroids, jnp.take(returned, where_to, axis=0)


def shards(new_rows, list_ids, rotation, centroids, prior_counts):
    groups, chips = lax.axis_size("grp"), lax.axis_size("chip")
    rows = new_rows.shape[0]
    per_owner = centroids.shape[0]
    capacity = max(8, 2 * rows // chips)
    me = lax.axis_index("grp").astype(I32).reshape(1)
    ids = list_ids.reshape(1, rows)
    ids = jnp.concatenate([ids] + [around(ids, "grp", k + 1) for k in range(groups - 1)], axis=0)
    place, spare, codes, *leaving = assign(
        me, ids, new_rows, chips, capacity, CORES * per_owner
    )
    codes = exchange(codes, "chip")
    guests = [around(v, "grp", k + 1) for k, v in enumerate(leaving)]
    send = pack(place, new_rows, rotation, guests, chips * capacity)
    far_codes = around(codes, "core", 1)
    too_many = jnp.maximum(jnp.max(codes), jnp.max(far_codes)) >= FULL
    new_centroids, own, back = by_chip(me, place, codes, far_codes, send, centroids, prior_counts)

    def slow():
        rotated = jnp.dot(new_rows, rotation, preferred_element_type=F32).astype(BF16)
        return by_owner(rotated, list_ids, centroids, prior_counts)

    return lax.cond(too_many, slow, lambda: (new_centroids, join(spare, own, back)))


def solution(mesh):
    groups, owners = mesh.devices.shape
    parts = Mesh(mesh.devices.reshape(groups, owners // CORES, CORES), ("grp", "chip", "core"))
    every = ("grp", "chip", "core")
    lst = ("chip", "core")
    return jax.shard_map(
        shards,
        mesh=parts,
        in_specs=(P(every, None), P(every), P(), P(lst, None), P(lst)),
        out_specs=(P(lst, None), P(every, None)),
        check_vma=False,
    )
```

```python
import functools

import jax
import jax.numpy as jnp
from jax import lax
from jax.experimental import pallas as pl
from jax.experimental.pallas import tpu as pltpu
from jax.sharding import Mesh, PartitionSpec as P

CONTRACT_LAST = (((1,), (1,)), ((), ()))
CONTRACT_FIRST = (((0,), (0,)), ((), ()))
BF16 = jnp.bfloat16
F32 = jnp.float32
I32 = jnp.int32
CORES = 2
SPARE = 32
EXTRA = 128
FULL = 4096


def hot(mask):
    return jnp.where(mask, 1.0, 0.0).astype(BF16)


def iota(shape, dim):
    return lax.broadcasted_iota(I32, shape, dim)


def whole(shape):
    return pl.BlockSpec(shape, lambda *i: (0,) * len(shape))


def params():
    return pltpu.CompilerParams(vmem_limit_bytes=48 * 2**20)


def assign_kernel(
    groups, chips, capacity, per_chip,
    me_ref, ids_ref, rows_ref, place_ref, spare_ref, codes_ref, *leaving_refs,
):
    me = me_ref[0]
    rows = ids_ref.shape[1]
    earlier = hot(iota((rows, rows), 0) < iota((rows, rows), 1))
    cap = float(capacity)
    ids = [ids_ref[pl.ds(lax.rem(me - j + groups, groups), 1), :] for j in range(groups)]
    chip = [v // per_chip for v in ids]
    local = [v - c * per_chip + 1 for v, c in zip(ids, chip)]
    member = [iota((chips, rows), 0) == c for c in chip]
    member_f = [jnp.where(m, 1.0, 0.0) for m in member]
    before = jnp.dot(
        jnp.concatenate(member_f, axis=0).astype(BF16), earlier, preferred_element_type=F32
    )
    count = [jnp.sum(m, axis=1, keepdims=True) for m in member_f]
    free = [jnp.maximum(cap - n, 0.0) for n in count]
    over = [jnp.maximum(n - cap, 0.0) for n in count]
    free_at, over_at = [jnp.zeros_like(count[0])], [jnp.zeros_like(count[0])]
    for j in range(groups):
        free_at.append(free_at[-1] + free[j])
        over_at.append(over_at[-1] + over[j])
    lost = jnp.sum(jnp.maximum(over_at[-1] - free_at[-1], 0.0), axis=0, keepdims=True)
    target, slot = [], []
    for j in range(groups):
        rank = before[j * chips : (j + 1) * chips]
        stays = rank < cap
        entry = rank - cap + over_at[j]
        goes_to = jnp.full_like(rank, -1.0)
        lands = jnp.zeros_like(rank)
        for i in range(groups):
            inside = (entry >= free_at[i]) & (entry < free_at[i + 1])
            goes_to = jnp.where(inside, float(i), goes_to)
            lands = jnp.where(inside, count[i] + entry - free_at[i], lands)
        goes_to = jnp.where(stays, float(j), goes_to)
        lands = jnp.where(stays, rank, lands)
        target.append(jnp.sum(jnp.where(member[j], goes_to, 0.0), axis=0, keepdims=True).astype(I32))
        slot.append(jnp.sum(jnp.where(member[j], lands, 0.0), axis=0, keepdims=True).astype(I32))
    moves = [
        jnp.where(target[j] == i, 1.0, 0.0) if i != j else jnp.zeros((1, rows), F32)
        for j in range(groups)
        for i in range(groups)
    ]
    moves = jnp.concatenate(moves, axis=0)
    queue = jnp.dot(moves.astype(BF16), earlier, preferred_element_type=F32)
    totals = jnp.sum(moves, axis=1, keepdims=True)
    lost = lost + jnp.sum(jnp.maximum(totals - float(SPARE), 0.0), axis=0, keepdims=True)

    place = jnp.full((1, rows), -1, I32)
    spare = jnp.full((1, rows), -1, I32)
    arriving = jnp.zeros((8, EXTRA), F32)
    codes = jnp.zeros(codes_ref.shape, F32)
    for j in range(groups):
        mine = me == j
        flat = chip[j] * capacity + slot[j]
        place = jnp.where(mine & (target[j] == j), flat, place)
        for i in range(groups):
            if i == j:
                continue
            shift = (i - j) % groups - 1
            at = queue[j * groups + i : j * groups + i + 1].astype(I32) + shift * SPARE
            leaves = target[j] == i
            spare = jnp.where(mine & leaves, at, spare)
            to_me = hot((iota((EXTRA, rows), 0) == at) & leaves & (me == i))
            value = flat + 1
            high = value // 32
            low = value - high * 32
            pair = jnp.where(iota((8, rows), 0) == 0, high, low).astype(F32).astype(BF16)
            arriving = arriving + lax.dot_general(
                pair, to_me, CONTRACT_LAST, preferred_element_type=F32
            )
        at_slot = hot(iota((capacity, rows), 0) == slot[j])
        served = member[j] & (target[j] == me)
        high = local[j] // 32
        low = local[j] - high * 32
        for value, factor in ((high, 32.0), (low, 1.0)):
            spread = jnp.where(served, value.astype(F32), 0.0).astype(BF16)
            codes = codes + factor * lax.dot_general(
                spread, at_slot, CONTRACT_LAST, preferred_element_type=F32
            )
    place_ref[:, :rows] = place
    place_ref[:, rows:] = (arriving[0:1] * 32.0 + arriving[1:2]).astype(I32) - 1
    spare_ref[...] = spare
    codes_ref[...] = (codes + jnp.where(lost > 0.0, float(FULL), 0.0)).astype(I32)
    for k, ref in enumerate(leaving_refs):
        chosen = hot(iota((SPARE, rows), 0) + k * SPARE == spare)
        ref[...] = jnp.dot(chosen, rows_ref[...], preferred_element_type=F32).astype(BF16)


def pack_kernel(block, place_ref, rows_ref, rotation_ref, a_ref, b_ref, c_ref, send_ref, all_ref):
    step = pl.program_id(0)
    rows = rows_ref.shape[0]

    @pl.when(step == 0)
    def _():
        def rotate(value):
            return jnp.dot(value, rotation_ref[...], preferred_element_type=F32).astype(BF16)

        guests = jnp.concatenate([a_ref[...], b_ref[...], c_ref[...]], axis=0)
        all_ref[:rows] = rotate(rows_ref[...])
        all_ref[rows : rows + 3 * SPARE] = rotate(guests)
        all_ref[rows + 3 * SPARE :] = jnp.zeros((EXTRA - 3 * SPARE, all_ref.shape[1]), BF16)

    chosen = hot(iota((block, all_ref.shape[0]), 0) + step * block == place_ref[...])
    send_ref[...] = jnp.dot(chosen, all_ref[...], preferred_element_type=F32).astype(BF16)


def pick_kernel(place_ref, returned_ref, own_ref, a_ref, b_ref, c_ref, chosen_ref):
    rows = own_ref.shape[0]

    @pl.when(pl.program_id(0) == 0)
    def _():
        chosen_ref[...] = hot(iota(chosen_ref.shape, 0) == place_ref[...])

    picked = lax.dot_general(
        chosen_ref[...], returned_ref[...], CONTRACT_FIRST, preferred_element_type=F32
    ).astype(BF16)
    own_ref[...] = picked[:rows]
    for k, ref in enumerate((a_ref, b_ref, c_ref)):
        ref[...] = picked[rows + k * SPARE : rows + (k + 1) * SPARE]


def join_kernel(spare_ref, own_ref, a_ref, b_ref, c_ref, out_ref):
    total = own_ref[...].astype(F32)
    spare = spare_ref[...]
    back = jnp.concatenate([a_ref[...], b_ref[...], c_ref[...]], axis=0)
    chosen = hot(iota((3 * SPARE, spare.shape[1]), 0) == spare)
    total = total + lax.dot_general(chosen, back, CONTRACT_FIRST, preferred_element_type=F32)
    out_ref[...] = total.astype(BF16)


def finish_kernel(made, me_ref, *refs):
    centroids_ref, *step_refs, out_ref = refs[made:]
    rows = out_ref.shape[0]
    for k, ref in enumerate(step_refs):

        @pl.when(pl.program_id(0) == k)
        def _(ref=ref):
            at = pl.ds(pl.multiple_of(pl.program_id(1) * rows, rows), rows)
            out_ref[...] = centroids_ref[...] + ref[at, :].astype(F32)


def shape(dims, dtype):
    return jax.ShapeDtypeStruct(dims, dtype)


def assign(me, ids, new_rows, chips, capacity, per_chip):
    groups, rows = ids.shape
    vmem = pl.BlockSpec(memory_space=pltpu.VMEM)
    return pl.pallas_call(
        functools.partial(assign_kernel, groups, chips, capacity, per_chip),
        in_specs=[pl.BlockSpec(memory_space=pltpu.SMEM), vmem, vmem],
        out_shape=(
            shape((1, rows + EXTRA), I32),
            shape((1, rows), I32),
            shape((chips, capacity), I32),
        )
        + (shape((SPARE, new_rows.shape[1]), BF16),) * 3,
        compiler_params=params(),
        name="assign",
    )(me, ids, new_rows)


def pack(place, new_rows, rotation, guests, slots):
    rows, width = new_rows.shape
    block = 256
    return pl.pallas_call(
        functools.partial(pack_kernel, block),
        grid=(slots // block,),
        in_specs=[whole(v.shape) for v in (place, new_rows, rotation, *guests)],
        out_specs=pl.BlockSpec((block, width), lambda i: (i, 0)),
        out_shape=shape((slots, width), BF16),
        scratch_shapes=[pltpu.VMEM((rows + EXTRA, width), BF16)],
        compiler_params=params(),
        name="pack",
    )(place, new_rows, rotation, *guests)


def pick(place, returned):
    slots, width = returned.shape
    rows = place.shape[1] - EXTRA
    block = 256

    def columns(count):
        return pl.BlockSpec((count, block), lambda i: (0, i))

    return pl.pallas_call(
        pick_kernel,
        grid=(width // block,),
        in_specs=[whole(place.shape), columns(slots)],
        out_specs=(columns(rows),) + (columns(SPARE),) * 3,
        out_shape=(shape((rows, width), BF16),) + (shape((SPARE, width), BF16),) * 3,
        scratch_shapes=[pltpu.VMEM((slots, place.shape[1]), BF16)],
        compiler_params=params(),
        name="pick",
    )(place, returned)


def join(spare, own, guests):
    return pl.pallas_call(
        join_kernel,
        out_shape=shape(own.shape, BF16),
        compiler_params=params(),
        name="join",
    )(spare, own, *guests)


def finish(me, made, centroids, steps, shift):
    groups = lax.axis_size("grp")
    quarter, width = steps[0].shape
    pieces = 2
    block = pl.BlockSpec(
        (quarter // pieces, width),
        lambda k, i, me: (lax.rem(me[0] - shift - k + groups, groups) * pieces + i, 0),
    )
    return pl.pallas_call(
        functools.partial(finish_kernel, len(made)),
        grid_spec=pltpu.PrefetchScalarGridSpec(
            num_scalar_prefetch=1,
            grid=(len(steps), pieces),
            in_specs=[pl.BlockSpec(memory_space=pl.ANY)] * len(made)
            + [block]
            + [whole(step.shape) for step in steps],
            out_specs=block,
        ),
        out_shape=pltpu.HBM(centroids.shape, F32),
        input_output_aliases={1: 0} if made else {},
        compiler_params=params(),
        name="finish",
    )(me, *made, centroids, *steps)


def around(value, axis, shift):
    count = lax.axis_size(axis)
    return lax.ppermute(value, axis, [(i, (i + shift) % count) for i in range(count)])


def exchange(value, axes):
    return lax.all_to_all(value, axes, split_axis=0, concat_axis=0, tiled=True)


def by_chip(me, place, codes, far_codes, send, centroids, prior_counts):
    groups, chips = lax.axis_size("grp"), lax.axis_size("chip")
    core = lax.axis_index("core")
    per_owner, width = centroids.shape
    slots = send.shape[0]
    capacity = slots // chips
    arrived = exchange(send.reshape(chips, capacity, width), "chip").reshape(slots, width)
    table = jnp.concatenate([centroids, around(centroids, "core", 1)], axis=0)

    def nearness(codes):
        local = codes.reshape(slots) - 1
        near = local % per_owner
        near = jnp.where(local // per_owner == core, near, near + per_owner)
        return jnp.where(local >= 0, near, -1)

    here = nearness(codes)
    lookup = jnp.take(table, jnp.maximum(here, 0), axis=0, mode="clip")
    quarter = per_owner // groups
    lists = (jnp.arange(per_owner, dtype=I32) + me * quarter) % per_owner
    both = jnp.concatenate([here, nearness(far_codes)])
    counts = jnp.sum(lists[:, None] == both[None, :], axis=1, dtype=F32)
    counts = [
        around(counts[k * quarter : (k + 1) * quarter], "grp", k) if k else counts[:quarter]
        for k in range(groups)
    ]
    own_prior = lax.dynamic_slice_in_dim(prior_counts, me[0] * quarter, quarter)
    total_counts = own_prior + sum(counts[1:], counts[0])
    arrived, lookup, total_counts = lax.optimization_barrier((arrived, lookup, total_counts))
    residual = lax.optimization_barrier((arrived.astype(F32) - lookup).astype(BF16))
    returned = exchange(residual.reshape(chips, capacity, width), "chip").reshape(slots, width)
    far_sums = jnp.dot(
        (lists[:, None] + per_owner == here[None, :]).astype(BF16),
        residual,
        preferred_element_type=F32,
    ).astype(BF16)
    far_sums = around(far_sums, "core", 1)
    sums = jnp.dot(
        (lists[:, None] == here[None, :]).astype(BF16), residual, preferred_element_type=F32
    )
    sums = (sums + far_sums.astype(F32)).astype(BF16)
    parts = [
        around(sums[k * quarter : (k + 1) * quarter], "grp", k) if k else sums[:quarter]
        for k in range(groups)
    ]
    total = parts[0].astype(F32)
    for part in parts[1:]:
        total = total + part.astype(F32)
    step = (total / total_counts[:, None]).astype(BF16)
    others = [around(step, "grp", k) for k in range(1, groups)]
    new_centroids = finish(me, (), centroids, [step], 0)
    returned, new_centroids = lax.optimization_barrier((returned, new_centroids))
    own, *back = pick(place, returned)
    back = [around(v, "grp", groups - k - 1) for k, v in enumerate(back)]
    new_centroids = finish(me, (new_centroids,), centroids, others, 1)
    return new_centroids, own, back


def by_owner(rotated, list_ids, centroids, prior_counts):
    lst = ("chip", "core")
    peers = lax.axis_size("chip") * CORES
    rows, width = rotated.shape
    per_owner = centroids.shape[0]
    capacity = max(2, 4 * rows // peers)
    slots = peers * capacity
    owner = list_ids // per_owner
    table = (owner[:, None] == jnp.arange(peers, dtype=I32)[None, :]).astype(I32)
    rank = jnp.sum(table * (jnp.cumsum(table, axis=0) - 1), axis=1)
    where_to = owner * capacity + rank
    source = jnp.full((slots,), rows, I32).at[where_to].set(jnp.arange(rows, dtype=I32))
    filled = source < rows
    safe = jnp.minimum(source, rows - 1)
    send = jnp.where(filled[:, None], jnp.take(rotated, safe, axis=0), jnp.zeros((), BF16))
    send_ids = jnp.where(filled, jnp.take(list_ids, safe, axis=0), -1)
    arrived = exchange(send.reshape(peers, capacity, width), lst).reshape(slots, width)
    arrived_ids = exchange(send_ids.reshape(peers, capacity), lst).reshape(slots)
    local = jnp.where(arrived_ids >= 0, arrived_ids - lax.axis_index(lst) * per_owner, -1)
    lookup = jnp.take(centroids, jnp.maximum(local, 0), axis=0)
    residual = jnp.where((local >= 0)[:, None], arrived.astype(F32) - lookup, 0.0).astype(BF16)
    member = (jnp.arange(per_owner, dtype=I32)[:, None] == local[None, :]).astype(BF16)
    sums = jnp.dot(member, residual, preferred_element_type=F32)
    counts = jnp.sum(member, axis=1, dtype=F32)
    total_sums = lax.psum(sums.astype(BF16), "grp").astype(F32)
    total_counts = prior_counts + lax.psum(counts, "grp")
    new_centroids = centroids + total_sums / total_counts[:, None]
    returned = exchange(residual.reshape(peers, capacity, width), lst).reshape(slots, width)
    return new_centroids, jnp.take(returned, where_to, axis=0)


def shards(new_rows, list_ids, rotation, centroids, prior_counts):
    groups, chips = lax.axis_size("grp"), lax.axis_size("chip")
    rows = new_rows.shape[0]
    per_owner = centroids.shape[0]
    capacity = max(8, 2 * rows // chips)
    me = lax.axis_index("grp").astype(I32).reshape(1)
    ids = list_ids.reshape(1, rows)
    ids = jnp.concatenate([ids] + [around(ids, "grp", k + 1) for k in range(groups - 1)], axis=0)
    place, spare, codes, *leaving = assign(
        me, ids, new_rows, chips, capacity, CORES * per_owner
    )
    codes = exchange(codes, "chip")
    guests = [around(v, "grp", k + 1) for k, v in enumerate(leaving)]
    send = pack(place, new_rows, rotation, guests, chips * capacity)
    far_codes = around(codes, "core", 1)
    too_many = jnp.maximum(jnp.max(codes), jnp.max(far_codes)) >= FULL
    new_centroids, own, back = by_chip(me, place, codes, far_codes, send, centroids, prior_counts)

    def slow():
        rotated = jnp.dot(new_rows, rotation, preferred_element_type=F32).astype(BF16)
        return by_owner(rotated, list_ids, centroids, prior_counts)

    return lax.cond(too_many, slow, lambda: (new_centroids, join(spare, own, back)))


def solution(mesh):
    groups, owners = mesh.devices.shape
    parts = Mesh(mesh.devices.reshape(groups, owners // CORES, CORES), ("grp", "chip", "core"))
    every = ("grp", "chip", "core")
    lst = ("chip", "core")
    return jax.shard_map(
        shards,
        mesh=parts,
        in_specs=(P(every, None), P(every), P(), P(lst, None), P(lst)),
        out_specs=(P(lst, None), P(every, None)),
        check_vma=False,
    )
```

```python
import functools

import jax
import jax.numpy as jnp
from jax import lax
from jax.experimental import pallas as pl
from jax.experimental.pallas import tpu as pltpu
from jax.sharding import Mesh, PartitionSpec as P

CONTRACT_LAST = (((1,), (1,)), ((), ()))
CONTRACT_FIRST = (((0,), (0,)), ((), ()))
BF16 = jnp.bfloat16
F32 = jnp.float32
I32 = jnp.int32
CORES = 2
SPARE = 32
EXTRA = 128
FULL = 4096


def hot(mask):
    return jnp.where(mask, 1.0, 0.0).astype(BF16)


def iota(shape, dim):
    return lax.broadcasted_iota(I32, shape, dim)


def whole(shape):
    return pl.BlockSpec(shape, lambda *i: (0,) * len(shape))


def params():
    return pltpu.CompilerParams(vmem_limit_bytes=48 * 2**20)


def assign_kernel(
    groups, chips, capacity, per_chip,
    me_ref, ids_ref, rows_ref, place_ref, spare_ref, codes_ref, *leaving_refs,
):
    me = me_ref[0]
    rows = ids_ref.shape[1]
    earlier = hot(iota((rows, rows), 0) < iota((rows, rows), 1))
    cap = float(capacity)
    ids = [ids_ref[pl.ds(lax.rem(me - j + groups, groups), 1), :] for j in range(groups)]
    chip = [v // per_chip for v in ids]
    local = [v - c * per_chip + 1 for v, c in zip(ids, chip)]
    member = [iota((chips, rows), 0) == c for c in chip]
    member_f = [jnp.where(m, 1.0, 0.0) for m in member]
    before = jnp.dot(
        jnp.concatenate(member_f, axis=0).astype(BF16), earlier, preferred_element_type=F32
    )
    count = [jnp.sum(m, axis=1, keepdims=True) for m in member_f]
    free = [jnp.maximum(cap - n, 0.0) for n in count]
    over = [jnp.maximum(n - cap, 0.0) for n in count]
    free_at, over_at = [jnp.zeros_like(count[0])], [jnp.zeros_like(count[0])]
    for j in range(groups):
        free_at.append(free_at[-1] + free[j])
        over_at.append(over_at[-1] + over[j])
    lost = jnp.sum(jnp.maximum(over_at[-1] - free_at[-1], 0.0), axis=0, keepdims=True)
    target, slot = [], []
    for j in range(groups):
        rank = before[j * chips : (j + 1) * chips]
        stays = rank < cap
        entry = rank - cap + over_at[j]
        goes_to = jnp.full_like(rank, -1.0)
        lands = jnp.zeros_like(rank)
        for i in range(groups):
            inside = (entry >= free_at[i]) & (entry < free_at[i + 1])
            goes_to = jnp.where(inside, float(i), goes_to)
            lands = jnp.where(inside, count[i] + entry - free_at[i], lands)
        goes_to = jnp.where(stays, float(j), goes_to)
        lands = jnp.where(stays, rank, lands)
        target.append(jnp.sum(jnp.where(member[j], goes_to, 0.0), axis=0, keepdims=True).astype(I32))
        slot.append(jnp.sum(jnp.where(member[j], lands, 0.0), axis=0, keepdims=True).astype(I32))
    moves = [
        jnp.where(target[j] == i, 1.0, 0.0) if i != j else jnp.zeros((1, rows), F32)
        for j in range(groups)
        for i in range(groups)
    ]
    moves = jnp.concatenate(moves, axis=0)
    queue = jnp.dot(moves.astype(BF16), earlier, preferred_element_type=F32)
    totals = jnp.sum(moves, axis=1, keepdims=True)
    lost = lost + jnp.sum(jnp.maximum(totals - float(SPARE), 0.0), axis=0, keepdims=True)

    place = jnp.full((1, rows), -1, I32)
    spare = jnp.full((1, rows), -1, I32)
    arriving = jnp.zeros((8, EXTRA), F32)
    codes = jnp.zeros(codes_ref.shape, F32)
    for j in range(groups):
        mine = me == j
        flat = chip[j] * capacity + slot[j]
        place = jnp.where(mine & (target[j] == j), flat, place)
        for i in range(groups):
            if i == j:
                continue
            shift = (i - j) % groups - 1
            at = queue[j * groups + i : j * groups + i + 1].astype(I32) + shift * SPARE
            leaves = target[j] == i
            spare = jnp.where(mine & leaves, at, spare)
            to_me = hot((iota((EXTRA, rows), 0) == at) & leaves & (me == i))
            value = flat + 1
            high = value // 32
            low = value - high * 32
            pair = jnp.where(iota((8, rows), 0) == 0, high, low).astype(F32).astype(BF16)
            arriving = arriving + lax.dot_general(
                pair, to_me, CONTRACT_LAST, preferred_element_type=F32
            )
        at_slot = hot(iota((capacity, rows), 0) == slot[j])
        served = member[j] & (target[j] == me)
        high = local[j] // 32
        low = local[j] - high * 32
        for value, factor in ((high, 32.0), (low, 1.0)):
            spread = jnp.where(served, value.astype(F32), 0.0).astype(BF16)
            codes = codes + factor * lax.dot_general(
                spread, at_slot, CONTRACT_LAST, preferred_element_type=F32
            )
    place_ref[:, :rows] = place
    place_ref[:, rows:] = (arriving[0:1] * 32.0 + arriving[1:2]).astype(I32) - 1
    spare_ref[...] = spare
    codes_ref[...] = (codes + jnp.where(lost > 0.0, float(FULL), 0.0)).astype(I32)
    for k, ref in enumerate(leaving_refs):
        chosen = hot(iota((SPARE, rows), 0) + k * SPARE == spare)
        ref[...] = jnp.dot(chosen, rows_ref[...], preferred_element_type=F32).astype(BF16)


def pack_kernel(block, place_ref, rows_ref, rotation_ref, a_ref, b_ref, c_ref, send_ref, all_ref):
    step = pl.program_id(0)
    rows = rows_ref.shape[0]

    @pl.when(step == 0)
    def _():
        def rotate(value):
            return jnp.dot(value, rotation_ref[...], preferred_element_type=F32).astype(BF16)

        guests = jnp.concatenate([a_ref[...], b_ref[...], c_ref[...]], axis=0)
        all_ref[:rows] = rotate(rows_ref[...])
        all_ref[rows : rows + 3 * SPARE] = rotate(guests)
        all_ref[rows + 3 * SPARE :] = jnp.zeros((EXTRA - 3 * SPARE, all_ref.shape[1]), BF16)

    chosen = hot(iota((block, all_ref.shape[0]), 0) + step * block == place_ref[...])
    send_ref[...] = jnp.dot(chosen, all_ref[...], preferred_element_type=F32).astype(BF16)


def pick_kernel(place_ref, returned_ref, own_ref, a_ref, b_ref, c_ref, chosen_ref):
    rows = own_ref.shape[0]

    @pl.when(pl.program_id(0) == 0)
    def _():
        chosen_ref[...] = hot(iota(chosen_ref.shape, 0) == place_ref[...])

    picked = lax.dot_general(
        chosen_ref[...], returned_ref[...], CONTRACT_FIRST, preferred_element_type=F32
    ).astype(BF16)
    own_ref[...] = picked[:rows]
    for k, ref in enumerate((a_ref, b_ref, c_ref)):
        ref[...] = picked[rows + k * SPARE : rows + (k + 1) * SPARE]


def join_kernel(spare_ref, own_ref, a_ref, b_ref, c_ref, out_ref):
    total = own_ref[...].astype(F32)
    spare = spare_ref[...]
    back = jnp.concatenate([a_ref[...], b_ref[...], c_ref[...]], axis=0)
    chosen = hot(iota((3 * SPARE, spare.shape[1]), 0) == spare)
    total = total + lax.dot_general(chosen, back, CONTRACT_FIRST, preferred_element_type=F32)
    out_ref[...] = total.astype(BF16)


def finish_kernel(made, me_ref, *refs):
    centroids_ref, *step_refs, out_ref = refs[made:]
    rows = out_ref.shape[0]
    for k, ref in enumerate(step_refs):

        @pl.when(pl.program_id(0) == k)
        def _(ref=ref):
            at = pl.ds(pl.multiple_of(pl.program_id(1) * rows, rows), rows)
            out_ref[...] = centroids_ref[...] + ref[at, :].astype(F32)


def shape(dims, dtype):
    return jax.ShapeDtypeStruct(dims, dtype)


def assign(me, ids, new_rows, chips, capacity, per_chip):
    groups, rows = ids.shape
    vmem = pl.BlockSpec(memory_space=pltpu.VMEM)
    return pl.pallas_call(
        functools.partial(assign_kernel, groups, chips, capacity, per_chip),
        in_specs=[pl.BlockSpec(memory_space=pltpu.SMEM), vmem, vmem],
        out_shape=(
            shape((1, rows + EXTRA), I32),
            shape((1, rows), I32),
            shape((chips, capacity), I32),
        )
        + (shape((SPARE, new_rows.shape[1]), BF16),) * 3,
        compiler_params=params(),
        name="assign",
    )(me, ids, new_rows)


def pack(place, new_rows, rotation, guests, slots):
    rows, width = new_rows.shape
    block = 256
    return pl.pallas_call(
        functools.partial(pack_kernel, block),
        grid=(slots // block,),
        in_specs=[whole(v.shape) for v in (place, new_rows, rotation, *guests)],
        out_specs=pl.BlockSpec((block, width), lambda i: (i, 0)),
        out_shape=shape((slots, width), BF16),
        scratch_shapes=[pltpu.VMEM((rows + EXTRA, width), BF16)],
        compiler_params=params(),
        name="pack",
    )(place, new_rows, rotation, *guests)


def pick(place, returned):
    slots, width = returned.shape
    rows = place.shape[1] - EXTRA
    block = 256

    def columns(count):
        return pl.BlockSpec((count, block), lambda i: (0, i))

    return pl.pallas_call(
        pick_kernel,
        grid=(width // block,),
        in_specs=[whole(place.shape), columns(slots)],
        out_specs=(columns(rows),) + (columns(SPARE),) * 3,
        out_shape=(shape((rows, width), BF16),) + (shape((SPARE, width), BF16),) * 3,
        scratch_shapes=[pltpu.VMEM((slots, place.shape[1]), BF16)],
        compiler_params=params(),
        name="pick",
    )(place, returned)


def join(spare, own, guests):
    return pl.pallas_call(
        join_kernel,
        out_shape=shape(own.shape, BF16),
        compiler_params=params(),
        name="join",
    )(spare, own, *guests)


def finish(me, made, centroids, steps, shift, half):
    groups = lax.axis_size("grp")
    quarter, width = steps[0].shape
    pieces = 2
    block = pl.BlockSpec(
        (quarter // pieces, width),
        lambda k, i, me: (lax.rem(me[0] - shift - k + groups, groups) * pieces + i, half),
    )
    return pl.pallas_call(
        functools.partial(finish_kernel, len(made)),
        grid_spec=pltpu.PrefetchScalarGridSpec(
            num_scalar_prefetch=1,
            grid=(len(steps), pieces),
            in_specs=[pl.BlockSpec(memory_space=pl.ANY)] * len(made)
            + [block]
            + [whole(step.shape) for step in steps],
            out_specs=block,
        ),
        out_shape=pltpu.HBM(centroids.shape, F32),
        input_output_aliases={1: 0} if made else {},
        compiler_params=params(),
        name="finish",
    )(me, *made, centroids, *steps)


def around(value, axis, shift):
    count = lax.axis_size(axis)
    return lax.ppermute(value, axis, [(i, (i + shift) % count) for i in range(count)])


def exchange(value, axes):
    return lax.all_to_all(value, axes, split_axis=0, concat_axis=0, tiled=True)


def quarters_around(value):
    groups = lax.axis_size("grp")
    quarter = value.shape[0] // groups
    return [value[:quarter]] + [
        around(value[k * quarter : (k + 1) * quarter], "grp", k) for k in range(1, groups)
    ]


def by_chip(me, place, codes, far_codes, send, centroids, prior_counts):
    groups, chips = lax.axis_size("grp"), lax.axis_size("chip")
    core = lax.axis_index("core")
    per_owner, width = centroids.shape
    slots = send.shape[0]
    capacity = slots // chips
    arrived = exchange(send.reshape(chips, capacity, width), "chip").reshape(slots, width)
    table = jnp.concatenate([centroids, around(centroids, "core", 1)], axis=0)

    def nearness(codes):
        local = codes.reshape(slots) - 1
        near = local % per_owner
        near = jnp.where(local // per_owner == core, near, near + per_owner)
        return jnp.where(local >= 0, near, -1)

    here = nearness(codes)
    lookup = jnp.take(table, jnp.maximum(here, 0), axis=0, mode="clip")
    quarter = per_owner // groups
    lists = (jnp.arange(per_owner, dtype=I32) + me * quarter) % per_owner
    both = jnp.concatenate([here, nearness(far_codes)])
    counts = jnp.sum(lists[:, None] == both[None, :], axis=1, dtype=F32)
    counts = [
        around(counts[k * quarter : (k + 1) * quarter], "grp", k) if k else counts[:quarter]
        for k in range(groups)
    ]
    own_prior = lax.dynamic_slice_in_dim(prior_counts, me[0] * quarter, quarter)
    total_counts = own_prior + sum(counts[1:], counts[0])
    arrived, lookup, total_counts = lax.optimization_barrier((arrived, lookup, total_counts))
    residual = lax.optimization_barrier((arrived.astype(F32) - lookup).astype(BF16))
    returned = exchange(residual.reshape(chips, capacity, width), "chip").reshape(slots, width)
    far_sums = jnp.dot(
        (lists[:, None] + per_owner == here[None, :]).astype(BF16),
        residual,
        preferred_element_type=F32,
    ).astype(BF16)
    far_sums = around(far_sums, "core", 1)
    sums = jnp.dot(
        (lists[:, None] == here[None, :]).astype(BF16), residual, preferred_element_type=F32
    )
    sums = (sums + far_sums.astype(F32)).astype(BF16)
    steps, others = [], []
    for half in range(2):
        parts = quarters_around(sums[:, half * width // 2 : (half + 1) * width // 2])
        if steps:
            parts[0] = lax.optimization_barrier((parts[0], steps[0]))[0]
        total = parts[0].astype(F32)
        for part in parts[1:]:
            total = total + part.astype(F32)
        steps.append((total / total_counts[:, None]).astype(BF16))
        others.append([around(steps[-1], "grp", k) for k in range(1, groups)])
    new_centroids = finish(me, (), centroids, steps[:1], 0, 0)
    new_centroids = finish(me, (new_centroids,), centroids, steps[1:], 0, 1)
    returned, new_centroids = lax.optimization_barrier((returned, new_centroids))
    own, *back = pick(place, returned)
    back = [around(v, "grp", groups - k - 1) for k, v in enumerate(back)]
    for half in range(2):
        new_centroids = finish(me, (new_centroids,), centroids, others[half], 1, half)
    return new_centroids, own, back


def by_owner(rotated, list_ids, centroids, prior_counts):
    lst = ("chip", "core")
    peers = lax.axis_size("chip") * CORES
    rows, width = rotated.shape
    per_owner = centroids.shape[0]
    capacity = max(2, 4 * rows // peers)
    slots = peers * capacity
    owner = list_ids // per_owner
    table = (owner[:, None] == jnp.arange(peers, dtype=I32)[None, :]).astype(I32)
    rank = jnp.sum(table * (jnp.cumsum(table, axis=0) - 1), axis=1)
    where_to = owner * capacity + rank
    source = jnp.full((slots,), rows, I32).at[where_to].set(jnp.arange(rows, dtype=I32))
    filled = source < rows
    safe = jnp.minimum(source, rows - 1)
    send = jnp.where(filled[:, None], jnp.take(rotated, safe, axis=0), jnp.zeros((), BF16))
    send_ids = jnp.where(filled, jnp.take(list_ids, safe, axis=0), -1)
    arrived = exchange(send.reshape(peers, capacity, width), lst).reshape(slots, width)
    arrived_ids = exchange(send_ids.reshape(peers, capacity), lst).reshape(slots)
    local = jnp.where(arrived_ids >= 0, arrived_ids - lax.axis_index(lst) * per_owner, -1)
    lookup = jnp.take(centroids, jnp.maximum(local, 0), axis=0)
    residual = jnp.where((local >= 0)[:, None], arrived.astype(F32) - lookup, 0.0).astype(BF16)
    member = (jnp.arange(per_owner, dtype=I32)[:, None] == local[None, :]).astype(BF16)
    sums = jnp.dot(member, residual, preferred_element_type=F32)
    counts = jnp.sum(member, axis=1, dtype=F32)
    total_sums = lax.psum(sums.astype(BF16), "grp").astype(F32)
    total_counts = prior_counts + lax.psum(counts, "grp")
    new_centroids = centroids + total_sums / total_counts[:, None]
    returned = exchange(residual.reshape(peers, capacity, width), lst).reshape(slots, width)
    return new_centroids, jnp.take(returned, where_to, axis=0)


def shards(new_rows, list_ids, rotation, centroids, prior_counts):
    groups, chips = lax.axis_size("grp"), lax.axis_size("chip")
    rows = new_rows.shape[0]
    per_owner = centroids.shape[0]
    capacity = max(8, 2 * rows // chips)
    me = lax.axis_index("grp").astype(I32).reshape(1)
    ids = list_ids.reshape(1, rows)
    ids = jnp.concatenate([ids] + [around(ids, "grp", k + 1) for k in range(groups - 1)], axis=0)
    place, spare, codes, *leaving = assign(
        me, ids, new_rows, chips, capacity, CORES * per_owner
    )
    codes = exchange(codes, "chip")
    guests = [around(v, "grp", k + 1) for k, v in enumerate(leaving)]
    send = pack(place, new_rows, rotation, guests, chips * capacity)
    far_codes = around(codes, "core", 1)
    too_many = jnp.maximum(jnp.max(codes), jnp.max(far_codes)) >= FULL
    new_centroids, own, back = by_chip(me, place, codes, far_codes, send, centroids, prior_counts)

    def slow():
        rotated = jnp.dot(new_rows, rotation, preferred_element_type=F32).astype(BF16)
        return by_owner(rotated, list_ids, centroids, prior_counts)

    return lax.cond(too_many, slow, lambda: (new_centroids, join(spare, own, back)))


def solution(mesh):
    groups, owners = mesh.devices.shape
    parts = Mesh(mesh.devices.reshape(groups, owners // CORES, CORES), ("grp", "chip", "core"))
    every = ("grp", "chip", "core")
    lst = ("chip", "core")
    return jax.shard_map(
        shards,
        mesh=parts,
        in_specs=(P(every, None), P(every), P(), P(lst, None), P(lst)),
        out_specs=(P(lst, None), P(every, None)),
        check_vma=False,
    )
```

```python
import functools

import jax
import jax.numpy as jnp
from jax import lax
from jax.experimental import pallas as pl
from jax.experimental.pallas import tpu as pltpu
from jax.sharding import Mesh, PartitionSpec as P

CONTRACT_LAST = (((1,), (1,)), ((), ()))
CONTRACT_FIRST = (((0,), (0,)), ((), ()))
BF16 = jnp.bfloat16
F32 = jnp.float32
I32 = jnp.int32
CORES = 2
SPARE = 32
EXTRA = 128
FULL = 4096


def hot(mask):
    return jnp.where(mask, 1.0, 0.0).astype(BF16)


def iota(shape, dim):
    return lax.broadcasted_iota(I32, shape, dim)


def whole(shape):
    return pl.BlockSpec(shape, lambda *i: (0,) * len(shape))


def params():
    return pltpu.CompilerParams(vmem_limit_bytes=48 * 2**20)


def assign_kernel(
    groups, chips, capacity, per_chip,
    me_ref, ids_ref, rows_ref, place_ref, spare_ref, codes_ref, *leaving_refs,
):
    me = me_ref[0]
    rows = ids_ref.shape[1]
    earlier = hot(iota((rows, rows), 0) < iota((rows, rows), 1))
    cap = float(capacity)
    ids = [ids_ref[pl.ds(lax.rem(me - j + groups, groups), 1), :] for j in range(groups)]
    chip = [v // per_chip for v in ids]
    local = [v - c * per_chip + 1 for v, c in zip(ids, chip)]
    member = [iota((chips, rows), 0) == c for c in chip]
    member_f = [jnp.where(m, 1.0, 0.0) for m in member]
    before = jnp.dot(
        jnp.concatenate(member_f, axis=0).astype(BF16), earlier, preferred_element_type=F32
    )
    count = [jnp.sum(m, axis=1, keepdims=True) for m in member_f]
    free = [jnp.maximum(cap - n, 0.0) for n in count]
    over = [jnp.maximum(n - cap, 0.0) for n in count]
    free_at, over_at = [jnp.zeros_like(count[0])], [jnp.zeros_like(count[0])]
    for j in range(groups):
        free_at.append(free_at[-1] + free[j])
        over_at.append(over_at[-1] + over[j])
    lost = jnp.sum(jnp.maximum(over_at[-1] - free_at[-1], 0.0), axis=0, keepdims=True)
    target, slot = [], []
    for j in range(groups):
        rank = before[j * chips : (j + 1) * chips]
        stays = rank < cap
        entry = rank - cap + over_at[j]
        goes_to = jnp.full_like(rank, -1.0)
        lands = jnp.zeros_like(rank)
        for i in range(groups):
            inside = (entry >= free_at[i]) & (entry < free_at[i + 1])
            goes_to = jnp.where(inside, float(i), goes_to)
            lands = jnp.where(inside, count[i] + entry - free_at[i], lands)
        goes_to = jnp.where(stays, float(j), goes_to)
        lands = jnp.where(stays, rank, lands)
        target.append(jnp.sum(jnp.where(member[j], goes_to, 0.0), axis=0, keepdims=True).astype(I32))
        slot.append(jnp.sum(jnp.where(member[j], lands, 0.0), axis=0, keepdims=True).astype(I32))
    moves = [
        jnp.where(target[j] == i, 1.0, 0.0) if i != j else jnp.zeros((1, rows), F32)
        for j in range(groups)
        for i in range(groups)
    ]
    moves = jnp.concatenate(moves, axis=0)
    queue = jnp.dot(moves.astype(BF16), earlier, preferred_element_type=F32)
    totals = jnp.sum(moves, axis=1, keepdims=True)
    lost = lost + jnp.sum(jnp.maximum(totals - float(SPARE), 0.0), axis=0, keepdims=True)

    place = jnp.full((1, rows), -1, I32)
    spare = jnp.full((1, rows), -1, I32)
    arriving = jnp.zeros((8, EXTRA), F32)
    codes = jnp.zeros(codes_ref.shape, F32)
    for j in range(groups):
        mine = me == j
        flat = chip[j] * capacity + slot[j]
        place = jnp.where(mine & (target[j] == j), flat, place)
        for i in range(groups):
            if i == j:
                continue
            shift = (i - j) % groups - 1
            at = queue[j * groups + i : j * groups + i + 1].astype(I32) + shift * SPARE
            leaves = target[j] == i
            spare = jnp.where(mine & leaves, at, spare)
            to_me = hot((iota((EXTRA, rows), 0) == at) & leaves & (me == i))
            value = flat + 1
            high = value // 32
            low = value - high * 32
            pair = jnp.where(iota((8, rows), 0) == 0, high, low).astype(F32).astype(BF16)
            arriving = arriving + lax.dot_general(
                pair, to_me, CONTRACT_LAST, preferred_element_type=F32
            )
        at_slot = hot(iota((capacity, rows), 0) == slot[j])
        served = member[j] & (target[j] == me)
        high = local[j] // 32
        low = local[j] - high * 32
        for value, factor in ((high, 32.0), (low, 1.0)):
            spread = jnp.where(served, value.astype(F32), 0.0).astype(BF16)
            codes = codes + factor * lax.dot_general(
                spread, at_slot, CONTRACT_LAST, preferred_element_type=F32
            )
    place_ref[:, :rows] = place
    place_ref[:, rows:] = (arriving[0:1] * 32.0 + arriving[1:2]).astype(I32) - 1
    spare_ref[...] = spare
    codes_ref[...] = (codes + jnp.where(lost > 0.0, float(FULL), 0.0)).astype(I32)
    for k, ref in enumerate(leaving_refs):
        chosen = hot(iota((SPARE, rows), 0) + k * SPARE == spare)
        ref[...] = jnp.dot(chosen, rows_ref[...], preferred_element_type=F32).astype(BF16)


def pack_kernel(block, place_ref, rows_ref, rotation_ref, a_ref, b_ref, c_ref, send_ref, all_ref):
    step = pl.program_id(0)
    rows = rows_ref.shape[0]

    @pl.when(step == 0)
    def _():
        def rotate(value):
            return jnp.dot(value, rotation_ref[...], preferred_element_type=F32).astype(BF16)

        guests = jnp.concatenate([a_ref[...], b_ref[...], c_ref[...]], axis=0)
        all_ref[:rows] = rotate(rows_ref[...])
        all_ref[rows : rows + 3 * SPARE] = rotate(guests)
        all_ref[rows + 3 * SPARE :] = jnp.zeros((EXTRA - 3 * SPARE, all_ref.shape[1]), BF16)

    chosen = hot(iota((block, all_ref.shape[0]), 0) + step * block == place_ref[...])
    send_ref[...] = jnp.dot(chosen, all_ref[...], preferred_element_type=F32).astype(BF16)


def pick_kernel(place_ref, returned_ref, own_ref, a_ref, b_ref, c_ref, chosen_ref):
    rows = own_ref.shape[0]

    @pl.when(pl.program_id(0) == 0)
    def _():
        chosen_ref[...] = hot(iota(chosen_ref.shape, 0) == place_ref[...])

    picked = lax.dot_general(
        chosen_ref[...], returned_ref[...], CONTRACT_FIRST, preferred_element_type=F32
    ).astype(BF16)
    own_ref[...] = picked[:rows]
    for k, ref in enumerate((a_ref, b_ref, c_ref)):
        ref[...] = picked[rows + k * SPARE : rows + (k + 1) * SPARE]


def join_kernel(spare_ref, own_ref, a_ref, b_ref, c_ref, out_ref):
    total = own_ref[...].astype(F32)
    spare = spare_ref[...]
    back = jnp.concatenate([a_ref[...], b_ref[...], c_ref[...]], axis=0)
    chosen = hot(iota((3 * SPARE, spare.shape[1]), 0) == spare)
    total = total + lax.dot_general(chosen, back, CONTRACT_FIRST, preferred_element_type=F32)
    out_ref[...] = total.astype(BF16)


def finish_kernel(made, me_ref, *refs):
    centroids_ref, *step_refs, out_ref = refs[made:]
    rows = out_ref.shape[0]
    for k, ref in enumerate(step_refs):

        @pl.when(pl.program_id(0) == k)
        def _(ref=ref):
            at = pl.ds(pl.multiple_of(pl.program_id(1) * rows, rows), rows)
            out_ref[...] = centroids_ref[...] + ref[at, :].astype(F32)


def shape(dims, dtype):
    return jax.ShapeDtypeStruct(dims, dtype)


def assign(me, ids, new_rows, chips, capacity, per_chip):
    groups, rows = ids.shape
    vmem = pl.BlockSpec(memory_space=pltpu.VMEM)
    return pl.pallas_call(
        functools.partial(assign_kernel, groups, chips, capacity, per_chip),
        in_specs=[pl.BlockSpec(memory_space=pltpu.SMEM), vmem, vmem],
        out_shape=(
            shape((1, rows + EXTRA), I32),
            shape((1, rows), I32),
            shape((chips, capacity), I32),
        )
        + (shape((SPARE, new_rows.shape[1]), BF16),) * 3,
        compiler_params=params(),
        name="assign",
    )(me, ids, new_rows)


def pack(place, new_rows, rotation, guests, slots):
    rows, width = new_rows.shape
    block = 256
    return pl.pallas_call(
        functools.partial(pack_kernel, block),
        grid=(slots // block,),
        in_specs=[whole(v.shape) for v in (place, new_rows, rotation, *guests)],
        out_specs=pl.BlockSpec((block, width), lambda i: (i, 0)),
        out_shape=shape((slots, width), BF16),
        scratch_shapes=[pltpu.VMEM((rows + EXTRA, width), BF16)],
        compiler_params=params(),
        name="pack",
    )(place, new_rows, rotation, *guests)


def pick(place, returned):
    slots, width = returned.shape
    rows = place.shape[1] - EXTRA
    block = 256

    def columns(count):
        return pl.BlockSpec((count, block), lambda i: (0, i))

    return pl.pallas_call(
        pick_kernel,
        grid=(width // block,),
        in_specs=[whole(place.shape), columns(slots)],
        out_specs=(columns(rows),) + (columns(SPARE),) * 3,
        out_shape=(shape((rows, width), BF16),) + (shape((SPARE, width), BF16),) * 3,
        scratch_shapes=[pltpu.VMEM((slots, place.shape[1]), BF16)],
        compiler_params=params(),
        name="pick",
    )(place, returned)


def join(spare, own, guests):
    return pl.pallas_call(
        join_kernel,
        out_shape=shape(own.shape, BF16),
        compiler_params=params(),
        name="join",
    )(spare, own, *guests)


def finish(me, made, centroids, steps, shift):
    groups = lax.axis_size("grp")
    quarter, width = steps[0].shape
    pieces = 2
    block = pl.BlockSpec(
        (quarter // pieces, width),
        lambda k, i, me: (lax.rem(me[0] - shift - k + groups, groups) * pieces + i, 0),
    )
    return pl.pallas_call(
        functools.partial(finish_kernel, len(made)),
        grid_spec=pltpu.PrefetchScalarGridSpec(
            num_scalar_prefetch=1,
            grid=(len(steps), pieces),
            in_specs=[pl.BlockSpec(memory_space=pl.ANY)] * len(made)
            + [block]
            + [whole(step.shape) for step in steps],
            out_specs=block,
        ),
        out_shape=pltpu.HBM(centroids.shape, F32),
        input_output_aliases={1: 0} if made else {},
        compiler_params=params(),
        name="finish",
    )(me, *made, centroids, *steps)


def around(value, axis, shift):
    count = lax.axis_size(axis)
    return lax.ppermute(value, axis, [(i, (i + shift) % count) for i in range(count)])


def exchange(value, axes):
    return lax.all_to_all(value, axes, split_axis=0, concat_axis=0, tiled=True)


def by_chip(me, place, codes, far_codes, send, centroids, prior_counts):
    groups, chips = lax.axis_size("grp"), lax.axis_size("chip")
    core = lax.axis_index("core")
    per_owner, width = centroids.shape
    slots = send.shape[0]
    capacity = slots // chips
    arrived = exchange(send.reshape(chips, capacity, width), "chip").reshape(slots, width)
    table = jnp.concatenate([centroids, around(centroids, "core", 1)], axis=0)

    def nearness(codes):
        local = codes.reshape(slots) - 1
        near = local % per_owner
        near = jnp.where(local // per_owner == core, near, near + per_owner)
        return jnp.where(local >= 0, near, -1)

    here = nearness(codes)
    lookup = jnp.take(table, jnp.maximum(here, 0), axis=0, mode="clip")
    quarter = per_owner // groups
    lists = (jnp.arange(per_owner, dtype=I32) + me * quarter) % per_owner
    both = jnp.concatenate([here, nearness(far_codes)])
    counts = jnp.sum(lists[:, None] == both[None, :], axis=1, dtype=F32)
    counts = [
        around(counts[k * quarter : (k + 1) * quarter], "grp", k) if k else counts[:quarter]
        for k in range(groups)
    ]
    own_prior = lax.dynamic_slice_in_dim(prior_counts, me[0] * quarter, quarter)
    total_counts = own_prior + sum(counts[1:], counts[0])
    arrived, lookup, total_counts = lax.optimization_barrier((arrived, lookup, total_counts))
    residual = lax.optimization_barrier((arrived.astype(F32) - lookup).astype(BF16))
    returned = exchange(residual.reshape(chips, capacity, width), "chip").reshape(slots, width)
    far_sums = jnp.dot(
        (lists[:, None] + per_owner == here[None, :]).astype(BF16),
        residual,
        preferred_element_type=F32,
    ).astype(BF16)
    far_sums = around(far_sums, "core", 1)
    sums = jnp.dot(
        (lists[:, None] == here[None, :]).astype(BF16), residual, preferred_element_type=F32
    )
    sums = (sums + far_sums.astype(F32)).astype(BF16)
    parts = [
        around(sums[k * quarter : (k + 1) * quarter], "grp", k) if k else sums[:quarter]
        for k in range(groups)
    ]
    total = parts[0].astype(F32)
    for part in parts[1:]:
        total = total + part.astype(F32)
    step = (total / total_counts[:, None]).astype(BF16)
    others = [around(step, "grp", k) for k in range(1, groups)]
    new_centroids = finish(me, (), centroids, [step], 0)
    returned, new_centroids = lax.optimization_barrier((returned, new_centroids))
    own, *back = pick(place, returned)
    back = [around(v, "grp", groups - k - 1) for k, v in enumerate(back)]
    new_centroids = finish(me, (new_centroids,), centroids, others[:1], 1)
    new_centroids = finish(me, (new_centroids,), centroids, others[1:], 2)
    return new_centroids, own, back


def by_owner(rotated, list_ids, centroids, prior_counts):
    lst = ("chip", "core")
    peers = lax.axis_size("chip") * CORES
    rows, width = rotated.shape
    per_owner = centroids.shape[0]
    capacity = max(2, 4 * rows // peers)
    slots = peers * capacity
    owner = list_ids // per_owner
    table = (owner[:, None] == jnp.arange(peers, dtype=I32)[None, :]).astype(I32)
    rank = jnp.sum(table * (jnp.cumsum(table, axis=0) - 1), axis=1)
    where_to = owner * capacity + rank
    source = jnp.full((slots,), rows, I32).at[where_to].set(jnp.arange(rows, dtype=I32))
    filled = source < rows
    safe = jnp.minimum(source, rows - 1)
    send = jnp.where(filled[:, None], jnp.take(rotated, safe, axis=0), jnp.zeros((), BF16))
    send_ids = jnp.where(filled, jnp.take(list_ids, safe, axis=0), -1)
    arrived = exchange(send.reshape(peers, capacity, width), lst).reshape(slots, width)
    arrived_ids = exchange(send_ids.reshape(peers, capacity), lst).reshape(slots)
    local = jnp.where(arrived_ids >= 0, arrived_ids - lax.axis_index(lst) * per_owner, -1)
    lookup = jnp.take(centroids, jnp.maximum(local, 0), axis=0)
    residual = jnp.where((local >= 0)[:, None], arrived.astype(F32) - lookup, 0.0).astype(BF16)
    member = (jnp.arange(per_owner, dtype=I32)[:, None] == local[None, :]).astype(BF16)
    sums = jnp.dot(member, residual, preferred_element_type=F32)
    counts = jnp.sum(member, axis=1, dtype=F32)
    total_sums = lax.psum(sums.astype(BF16), "grp").astype(F32)
    total_counts = prior_counts + lax.psum(counts, "grp")
    new_centroids = centroids + total_sums / total_counts[:, None]
    returned = exchange(residual.reshape(peers, capacity, width), lst).reshape(slots, width)
    return new_centroids, jnp.take(returned, where_to, axis=0)


def shards(new_rows, list_ids, rotation, centroids, prior_counts):
    groups, chips = lax.axis_size("grp"), lax.axis_size("chip")
    rows = new_rows.shape[0]
    per_owner = centroids.shape[0]
    capacity = max(8, 2 * rows // chips)
    me = lax.axis_index("grp").astype(I32).reshape(1)
    ids = list_ids.reshape(1, rows)
    ids = jnp.concatenate([ids] + [around(ids, "grp", k + 1) for k in range(groups - 1)], axis=0)
    place, spare, codes, *leaving = assign(
        me, ids, new_rows, chips, capacity, CORES * per_owner
    )
    codes = exchange(codes, "chip")
    guests = [around(v, "grp", k + 1) for k, v in enumerate(leaving)]
    send = pack(place, new_rows, rotation, guests, chips * capacity)
    far_codes = around(codes, "core", 1)
    too_many = jnp.maximum(jnp.max(codes), jnp.max(far_codes)) >= FULL
    new_centroids, own, back = by_chip(me, place, codes, far_codes, send, centroids, prior_counts)

    def slow():
        rotated = jnp.dot(new_rows, rotation, preferred_element_type=F32).astype(BF16)
        return by_owner(rotated, list_ids, centroids, prior_counts)

    return lax.cond(too_many, slow, lambda: (new_centroids, join(spare, own, back)))


def solution(mesh):
    groups, owners = mesh.devices.shape
    parts = Mesh(mesh.devices.reshape(groups, owners // CORES, CORES), ("grp", "chip", "core"))
    every = ("grp", "chip", "core")
    lst = ("chip", "core")
    return jax.shard_map(
        shards,
        mesh=parts,
        in_specs=(P(every, None), P(every), P(), P(lst, None), P(lst)),
        out_specs=(P(lst, None), P(every, None)),
        check_vma=False,
    )
```
